128 devices in a mesh: dp: 4 (over y_hi, core), expert: 32 (over x, y_lo, z).
Axes of the slice: x: 4, y: 4 (y_hi: 2, y_lo: 2; y = y_hi * 2 + y_lo), z: 4, core: 2. Of those that a mesh axis runs over, the one named last changes fastest.
Arguments:
- tokens: bfloat16 [16384, 2048], P(('dp', 'expert')), may hold values from -6 to 6
- routes: int32 [16384, 6], P(('dp', 'expert')), may hold values from 0 to 63, all different within a row; in each aligned block of 128 rows (0 to 127, 128 to 255, ...) at most 16 rows name the same one
- gates: bfloat16 [16384, 6], P(('dp', 'expert')), may hold values from 0.099609375 to 1
- out_grad: bfloat16 [16384, 2048], P(('dp', 'expert')), may hold values from -3 to 3
- expert_gate_up: bfloat16 [64, 2048, 1408], P('expert'), may hold values from -0.125 to 0.125
- expert_down: bfloat16 [64, 704, 2048], P('expert'), may hold values from -0.21875 to 0.21875
- moving_slot: int32 [32], replicated, may hold values from 0 to 1
Outputs:
- mixed: bfloat16 [16384, 2048], P(('dp', 'expert'))
- token_grad: bfloat16 [16384, 2048], P(('dp', 'expert'))
- gate_up_grad: bfloat16 [64, 2048, 1408], P('expert', 'dp')
- down_grad: bfloat16 [64, 704, 2048], P('expert', None, 'dp')
The draws below stay inside these ranges and needn't reach their ends.
Inputs may be any that keep to these rules, and one draw needn't show every extreme that they name: `routes`: each row names 6 different experts; among the rows of one device no expert is named more than 16 times, a bound that some block reaches.
All inputs are finite; a program needn't handle non-finite values.
Results may differ from the reference program's by a relative error of at most 0.012.
Values may be sent and summed in bfloat16 or wider, within the bound.
A program may use at most 192 MiB of HBM per device.

```python
import math
import jax
import jax.numpy as jnp
import numpy as np
from jax import lax

D = 2048
FF = 704
TOP = 6
EXP_DEV = 2
TOK_DEV = 128
HOSTS = 32
EXPERTS = 64
CAP = 16
TOKENS = 16384
N_DP = 4


def plant(entries, key, least, high):
    extent = entries.shape
    spot = [jax.random.randint(jax.random.fold_in(key, axis), (), 0, extent[axis]) for axis in range(len(extent))]
    entries = entries.at[tuple(spot)].set(least)
    longest = extent.index(max(extent))
    spot[longest] = (spot[longest] + 1) % extent[longest]
    return entries.at[tuple(spot)].set(high)


def level_of(key, extent, shards, smallest, largest):
    gain, own = 1.0, jax.random.fold_in(key, 6)
    for position, shards_of in shards:
        draws = jnp.exp(jax.random.uniform(jax.random.fold_in(own, position), (shards_of,), jnp.float32, smallest / len(shards), largest / len(shards)))
        gain = gain * jnp.repeat(draws, extent[position] // shards_of).reshape([-1 if axis == position else 1 for axis in range(len(extent))])
    return gain


def routed_block(own_key, own, number, rows, count, top, reach, slope):
    sequence = jax.random.permutation(own_key, count)
    packed, common = shares(count, rows * top, reach, slope, True), shares(count, rows * top, reach, slope, False)
    places = jnp.arange(count)

    def named(lengths, turn):
        used = int((lengths > 0).sum())
        fixed = max(1, used // 4)
        passed = fixed + (places - fixed + turn * (used - fixed)) % max(1, count - fixed)
        return jnp.zeros((count,), jnp.int32).at[sequence[jnp.where(places < fixed, places, passed)]].set(jnp.asarray(lengths, jnp.int32))

    lengths = jnp.where(number % 4 == 0, named(packed, number // 4), named(common, number - number // 4 - 1))
    mixed = jax.random.permutation(jax.random.fold_in(own, 3), count)
    giver, sink = mixed[0:count // 2 * 2:2], mixed[1:count // 2 * 2:2]
    margin = jnp.minimum(lengths[giver] - 1, reach - lengths[sink]) // 2
    margin = jnp.where((giver == sequence[0]) | (sink == sequence[0]) | (lengths[sink] == 0), 0, jnp.maximum(margin, 0))
    passed = jax.random.randint(jax.random.fold_in(own, 4), (count // 2,), 0, 1 << 20) % (margin + 1)
    lengths = lengths.at[giver].add(-passed).at[sink].add(passed)
    members = jnp.searchsorted(jnp.cumsum(lengths), jnp.arange(rows * top), side="right").astype(jnp.int32)
    grid = members.reshape(top, rows).T
    grid = grid[jax.random.permutation(jax.random.fold_in(own, 1), rows)]
    turn = jax.random.randint(jax.random.fold_in(own, 2), (rows, 1), 0, top)
    return jnp.take_along_axis(grid, (jnp.arange(top)[None, :] + turn) % top, axis=1)


def shares(number_of, total, bound, slope, full):
    portions = [(1 << 20) // math.isqrt(rank ** slope) + 1 for rank in range(1, number_of + 1)]
    largest = bound if full else min(bound, max(-(-total // number_of), total * portions[0] // sum(portions)))
    least = 1 if total - largest >= number_of - 1 else 0
    given, surplus = [largest] + [least] * (number_of - 1), total - largest - least * (number_of - 1)
    while surplus > 0:
        free = [i for i in range(1, number_of) if given[i] < largest] or [i for i in range(1, number_of) if given[i] < bound]
        whole, remaining = sum([portions[i] for i in free]), surplus
        for i in free:
            addition = min(bound - given[i], max(1, remaining * portions[i] // whole), surplus)
            given[i] = given[i] + addition
            surplus = surplus - addition
    return np.array(given)


def centred(stream_key, dims, scale, bound, cuts=(), kind=jnp.bfloat16):
    entries = jax.random.normal(stream_key, dims, jnp.float32) * scale
    if len(cuts) > 0:
        entries = level_of(stream_key, dims, cuts, -0.22, 0.18) * entries
    return jnp.clip(entries, min=-bound, max=bound).astype(kind)


def setup_inputs(seed: int = 0) -> dict:
    keys = jax.random.split(jax.random.key(seed), 8)
    tokens = centred(keys[0], (TOKENS, D), 1.0, 6.0, ((0, 128),))
    routes_keys = jax.random.split(jax.random.fold_in(keys[1], 1), TOKENS // TOK_DEV)
    routes_turns = jax.random.permutation(jax.random.fold_in(keys[1], 3), TOKENS // TOK_DEV)
    routes = jax.vmap(lambda own, number: routed_block(jax.random.fold_in(keys[1], 2), own, number, TOK_DEV, EXPERTS, TOP, CAP, 2))(routes_keys, routes_turns).reshape((TOKENS, TOP))
    gates = jnp.clip(0.099609375 + 0.9003906 * jax.random.uniform(keys[2], (TOKENS, TOP), jnp.float32) ** level_of(keys[2], (TOKENS, TOP), ((0, 128),), -0.2, 0.2), 0.099609375, 1.0).astype(jnp.bfloat16)
    out_grad = centred(keys[3], (TOKENS, D), 0.5, 3.0, ((0, 128),))
    expert_gate_up = centred(keys[4], (EXPERTS, D, 2 * FF), D ** -0.5, 0.125, ((0, 32),))
    expert_down = centred(keys[5], (EXPERTS, FF, D), FF ** -0.5, 0.21875, ((0, 32),))
    moving_slot = plant(jax.random.randint(keys[6], (HOSTS,), 0, EXP_DEV), jax.random.fold_in(keys[6], 1), 0, EXP_DEV - 1).astype(jnp.int32)
    return {"tokens": tokens, "routes": routes, "gates": gates, "out_grad": out_grad, "expert_gate_up": expert_gate_up, "expert_down": expert_down, "moving_slot": moving_slot}


def expert_step(stack_in, scaled_cot, gate_up, down_proj):
    projected = jnp.dot(stack_in, gate_up, preferred_element_type=jnp.float32)
    pre_gate = projected[:, :FF]
    pre_up = projected[:, FF:]
    sigmoid_gate = jax.nn.sigmoid(pre_gate)
    activated = pre_gate * sigmoid_gate
    hidden = (activated * pre_up).astype(jnp.bfloat16)
    expert_out = jnp.dot(hidden, down_proj, preferred_element_type=jnp.float32).astype(jnp.bfloat16)
    hidden_grad = jnp.dot(scaled_cot, down_proj.T, preferred_element_type=jnp.float32)
    grad_gate = hidden_grad * pre_up * sigmoid_gate * (1.0 + pre_gate * (1.0 - sigmoid_gate))
    grad_up = hidden_grad * activated
    pre_grad = jnp.concatenate([grad_gate, grad_up], axis=1).astype(jnp.bfloat16)
    row_grad = jnp.dot(pre_grad, gate_up.T, preferred_element_type=jnp.float32).astype(jnp.bfloat16)
    return hidden, pre_grad, expert_out, row_grad


def sum_replicas(parts):
    rounded = lax.optimization_barrier(parts.astype(jnp.bfloat16))
    return jnp.sum(rounded.astype(jnp.float32), axis=0).astype(jnp.bfloat16)


def reference(tokens, routes, gates, out_grad, expert_gate_up, expert_down, moving_slot):
    blocks = TOKENS // TOK_DEV
    pairs = TOK_DEV * TOP
    replica_rows = HOSTS * CAP
    route_blocks = routes.reshape(blocks, pairs)
    gate_blocks = gates.reshape(blocks, pairs)
    block_ids = jnp.arange(blocks, dtype=jnp.int32)
    pair_ids = jnp.broadcast_to(jnp.arange(pairs, dtype=jnp.int32)[None, :], (blocks, pairs))
    slot_ids = jnp.arange(CAP, dtype=jnp.int32)

    def one_expert(carry, inputs):
        mixed_acc, grad_acc = carry
        expert_id, gate_up, down_proj = inputs
        matches = route_blocks == expert_id
        ranks = jnp.cumsum(matches.astype(jnp.int32), axis=1) - 1
        columns = jnp.where(matches, ranks, CAP).astype(jnp.int32)
        slot_table = jnp.zeros((blocks, CAP + 1), jnp.int32).at[block_ids[:, None], columns].set(pair_ids)[:, :CAP]
        counts = jnp.sum(matches.astype(jnp.int32), axis=1)
        is_live = slot_ids[None, :] < counts[:, None]
        token_rows = (block_ids[:, None] * TOK_DEV + slot_table // TOP).reshape(-1).astype(jnp.int32)
        slot_gates = jnp.where(is_live, jnp.take_along_axis(gate_blocks, slot_table, axis=1), 0).reshape(-1)
        live_flat = is_live.reshape(-1)
        stack_in = jnp.where(live_flat[:, None], tokens[token_rows], 0)
        cot_rows = jnp.where(live_flat[:, None], out_grad[token_rows], 0)
        scaled_cot = (slot_gates.astype(jnp.float32)[:, None] * cot_rows.astype(jnp.float32)).astype(jnp.bfloat16)
        hidden, pre_grad, expert_out, row_grad = expert_step(stack_in, scaled_cot, gate_up, down_proj)
        mixed_acc = mixed_acc.at[token_rows].add(slot_gates.astype(jnp.float32)[:, None] * expert_out.astype(jnp.float32))
        grad_acc = grad_acc.at[token_rows].add(row_grad.astype(jnp.float32))
        hidden_rep = hidden.reshape(N_DP, replica_rows, FF).astype(jnp.float32)
        cot_rep = scaled_cot.reshape(N_DP, replica_rows, D).astype(jnp.float32)
        input_rep = stack_in.reshape(N_DP, replica_rows, D).astype(jnp.float32)
        pre_rep = pre_grad.reshape(N_DP, replica_rows, 2 * FF).astype(jnp.float32)
        down_parts = jnp.einsum('rnf,rnd->rfd', hidden_rep, cot_rep)
        gate_up_parts = jnp.einsum('rnd,rnf->rdf', input_rep, pre_rep)
        return (mixed_acc, grad_acc), (sum_replicas(gate_up_parts), sum_replicas(down_parts))

    start = (jnp.zeros((TOKENS, D), jnp.float32), jnp.zeros((TOKENS, D), jnp.float32))
    expert_ids = jnp.arange(EXPERTS, dtype=jnp.int32)
    (mixed_acc, grad_acc), (gate_up_all, down_all) = lax.scan(one_expert, start, (expert_ids, expert_gate_up, expert_down))
    host_ids = jnp.arange(HOSTS, dtype=jnp.int32)
    partner = jnp.bitwise_xor(host_ids, HOSTS // 2)
    local_slots = jnp.arange(EXP_DEV, dtype=jnp.int32)
    moved = local_slots[None, :] == moving_slot[:, None]
    held = jnp.where(moved, EXP_DEV * partner[:, None] + moving_slot[partner][:, None], EXP_DEV * host_ids[:, None] + local_slots[None, :]).reshape(-1).astype(jnp.int32)
    return mixed_acc.astype(jnp.bfloat16), grad_acc.astype(jnp.bfloat16), gate_up_all[held], down_all[held]
```

```python
import jax
import jax.numpy as jnp
from jax import lax
from jax.experimental import pallas as pl
from jax.experimental.pallas import tpu as pltpu
from jax.sharding import PartitionSpec as P

MESH = pl.DeviceIdType.MESH
BF, F32 = jnp.bfloat16, jnp.float32

ROWS, WIDTH, HID, TOP, CAP = 128, 2048, 704, 6, 16
FULL = 2 * HID
QUARTER = WIDTH // 4

OUTBOUND = ((0, 1, 2, 0, 640), (1, 2, 0, 640, 640), (2, 0, 1, 1280, 768))
INBOUND = ((0, 1, 2, 0, 640), (1, 2, 0, 640, 640), (2, 0, 1, 1280, 768))


def device_at(x, y, z, core):
    return ((y // 2) * 2 + core, x * 8 + (y % 2) * 4 + z)


def dot(a, b, contract):
    return lax.dot_general(a, b, ((contract[:1], contract[1:]), ((), ())), preferred_element_type=F32)


def kernel(
    moving, tokens, routes, gates, out_grad, gate_up, down,
    mixed, token_grad, stay_gu, stay_dn, got_gu, got_dn, fwd1, fwd2, bck1, bck2,
    near1, near2, pick1, pick2, slot1, slot2, w_gu, w_dn, pre, hid, pre_grad,
    back1, back2, part1, part2, core_gu, core_dn, lane_gu, lane_dn, info, onehot, gated,
    sends, recvs, info_send, info_recv, local_sem, w_sem, grad_send, grad_recv, out_sem,
):
    dp, ex = lax.axis_index("dp"), lax.axis_index("expert")
    y_hi, core = dp // 2, dp % 2
    me = (ex // 8, y_hi * 2 + (ex // 4) % 2, ex % 4)

    def along(axis, step):
        place = list(me)
        place[axis] = (place[axis] + step) % 4
        return device_at(*place, core)

    other_core = device_at(*me, 1 - core)

    barrier = pltpu.get_barrier_semaphore()
    for axis in range(3):
        for step in (1, 2, 3):
            pl.semaphore_signal(barrier, inc=1, device_id=along(axis, step), device_id_type=MESH)
    pl.semaphore_signal(barrier, inc=1, device_id=other_core, device_id_type=MESH)

    load_gu = pltpu.make_async_copy(gate_up.at[y_hi], w_gu, w_sem.at[0])
    load_dn = pltpu.make_async_copy(down.at[y_hi], w_dn, w_sem.at[1])
    load_gu.start()
    load_dn.start()
    pl.semaphore_wait(barrier, 10)

    def send(src, dst, send_sem, recv_sem, device):
        copy = pltpu.make_async_remote_copy(
            src_ref=src, dst_ref=dst, send_sem=send_sem, recv_sem=recv_sem,
            device_id=device, device_id_type=MESH,
        )
        copy.start()
        return copy

    def keep(src, dst, sem):
        copy = pltpu.make_async_copy(src, dst, sem)
        copy.start()
        return copy

    def wait_all(copies):
        for copy in copies:
            copy.wait()

    def fixed(axis, index, ref, columns):
        spot = [slice(None)] * 3
        spot[axis] = index
        return ref.at[(*spot, slice(None), columns)]

    def gather_axis(stage, source, near):
        started = []
        for q, (a, _, _, first, count) in enumerate(OUTBOUND):
            columns = pl.ds(first, count)
            started.append([
                send(source.at[:, columns], near.at[step, :, columns],
                     sends.at[stage, q, step - 1], recvs.at[stage, q, step - 1], along(a, step))
                for step in (1, 3, 2)
            ])
        return started

    gather1 = gather_axis(0, tokens, near1)

    lane = lax.broadcasted_iota(jnp.int32, (ROWS, 128), 1)
    name = lane % 64
    hits = jnp.zeros((ROWS, 128), F32)
    weight = jnp.zeros((ROWS, 128), F32)
    all_routes, all_gates = routes[...], gates[...].astype(F32)
    for k in range(TOP):
        same = all_routes[:, k : k + 1] == name
        hits = hits + jnp.where(same, 1.0, 0.0)
        weight = weight + jnp.where(same, all_gates[:, k : k + 1], 0.0)
    below = lax.broadcasted_iota(jnp.int32, (ROWS, ROWS), 1) < lax.broadcasted_iota(
        jnp.int32, (ROWS, ROWS), 0
    )
    rank = dot(jnp.where(below, 1.0, 0.0).astype(BF), hits.astype(BF), (1, 0))
    own_info = jnp.where(lane < 64, jnp.where(hits > 0.5, rank, 99.0), weight).astype(BF)
    for axis in range(3):
        info[axis, 0] = own_info
    info_copies = [
        [
            send(info.at[axis, 0], info.at[axis, step],
                 info_send.at[axis, step - 1], info_recv.at[axis, step - 1], along(axis, step))
            for step in (1, 3, 2)
        ]
        for axis in range(3)
    ]
    gather2 = gather_axis(1, out_grad, near2)
    near1[0] = tokens[...]
    near2[0] = out_grad[...]

    def pick_masks(axis, b, c):
        row = lax.broadcasted_iota(jnp.int32, (128, 256), 0)
        column = lax.broadcasted_iota(jnp.int32, (128, 256), 1)
        place = [None, None, None]
        place[axis], place[b], place[c] = me[axis], column // 64, (column // 16) % 4
        expert = 2 * (place[0] * 8 + (place[1] % 2) * 4 + place[2]) + place[1] // 2
        choose_rank = jnp.where(row == expert, 1.0, 0.0).astype(BF)
        choose_gate = jnp.where(row == expert + 64, 1.0, 0.0).astype(BF)
        number = (lax.broadcasted_iota(jnp.int32, (ROWS, 256), 1) % 16).astype(F32)

        def one(step, _):
            ranks = dot(info[axis, step], choose_rank, (1, 0))
            scale = dot(info[axis, step], choose_gate, (1, 0))
            live = ranks == number
            onehot[axis, step] = jnp.where(live, 1.0, 0.0).astype(BF)
            gated[axis, step] = jnp.where(live, scale, 0.0).astype(BF)
            return 0

        lax.fori_loop(0, 4, one, 0)

    def pick(chunk, near, masks, picked):
        a, _, _, first, count = chunk

        def one(step, _):
            rows = dot(masks[a, step], near[step, :, first : first + count], (0, 0))
            source = (me[a] - step + 4) % 4
            picked[:, :, source, :, first : first + count] = rows.astype(BF).reshape(4, 4, 16, count)
            return 0

        lax.fori_loop(0, 4, one, 0)

    def second_axis(stage, q, picked, onward):
        a, b, _, first, count = OUTBOUND[q]
        columns = pl.ds(first, count)
        landing = (
            onward.at[:, :, me[b], :, columns] if a < b else onward.at[:, me[b], :, :, columns]
        )
        copies = [
            send(picked.at[(me[b] + step) % 4, :, :, :, columns], landing,
                 sends.at[stage, q, step - 1], recvs.at[stage, q, step - 1], along(b, step))
            for step in (1, 3, 2)
        ]
        copies.append(keep(picked.at[me[b], :, :, :, columns], landing, local_sem.at[stage, q]))
        return copies

    def third_axis(stage, q, onward, slots):
        _, _, c, first, count = OUTBOUND[q]
        columns = pl.ds(first, count)
        landing = fixed(c, me[c], slots, columns)
        copies = [
            send(onward.at[(me[c] + step) % 4, :, :, :, columns], landing,
                 sends.at[stage, q, step - 1], recvs.at[stage, q, step - 1], along(c, step))
            for step in (1, 3, 2)
        ]
        copies.append(keep(onward.at[me[c], :, :, :, columns], landing, local_sem.at[stage, q]))
        return copies

    spread1, spread2, final1, final2 = [], [], [], []
    for q, chunk in enumerate(OUTBOUND):
        wait_all(info_copies[chunk[0]])
        pick_masks(chunk[0], chunk[1], chunk[2])
        wait_all(gather1[q])
        pick(chunk, near1, onehot, pick1)
        spread1.append(second_axis(2, q, pick1, fwd1))
    for q, chunk in enumerate(OUTBOUND):
        wait_all(gather2[q])
        pick(chunk, near2, gated, pick2)
        spread2.append(second_axis(3, q, pick2, fwd2))
    for q in range(len(OUTBOUND)):
        wait_all(spread1[q])
        final1.append(third_axis(4, q, fwd1, slot1))
    for q in range(len(OUTBOUND)):
        wait_all(spread2[q])
        final2.append(third_axis(5, q, fwd2, slot2))

    load_gu.wait()
    load_dn.wait()
    for copies in final1:
        wait_all(copies)

    def forward(m, _):
        rows = slot1[m].reshape(256, WIDTH)
        projected = dot(rows, w_gu[...], (1, 0))
        here = pl.ds(pl.multiple_of(m * 256, 256), 256)
        pre[here] = projected
        pre_gate = projected[:, :HID]
        pre_up = projected[:, HID:]
        hidden = (pre_gate * jax.nn.sigmoid(pre_gate) * pre_up).astype(BF)
        hid[here] = hidden
        pick1[m] = dot(hidden, w_dn[...], (1, 0)).astype(BF).reshape(4, 4, 16, WIDTH)
        return 0

    lax.fori_loop(0, 4, forward, 0)

    def first_back(stage, result, onward):
        started = []
        for q, (_, _, c, first, count) in enumerate(INBOUND):
            columns = pl.ds(first, count)
            landing = onward.at[me[c], :, :, :, columns]
            copies = [
                send(fixed(c, (me[c] + step) % 4, result, columns), landing,
                     sends.at[stage, q, step - 1], recvs.at[stage, q, step - 1], along(c, step))
                for step in (1, 3, 2)
            ]
            copies.append(keep(fixed(c, me[c], result, columns), landing, local_sem.at[stage, q]))
            started.append(copies)
        return started

    def second_back(stage, q, onward, back):
        a, b, _, first, count = INBOUND[q]
        columns = pl.ds(first, count)

        def to(index):
            return onward.at[:, :, index, :, columns] if a < b else onward.at[:, index, :, :, columns]

        landing = back.at[me[b], :, :, :, columns]
        copies = [
            send(to((me[b] + step) % 4), landing,
                 sends.at[stage, q, step - 1], recvs.at[stage, q, step - 1], along(b, step))
            for step in (1, 3, 2)
        ]
        copies.append(keep(to(me[b]), landing, local_sem.at[stage, q]))
        return copies

    def combine(stage, q, back, masks, near, part):
        a, _, _, first, count = INBOUND[q]

        def one(step, _):
            target = (me[a] + step) % 4
            rows = back[:, :, target, :, first : first + count].reshape(256, count)
            near[step, :, first : first + count] = dot(
                masks[a, (4 - step) % 4], rows, (1, 0)
            ).astype(BF)
            return 0

        lax.fori_loop(0, 4, one, 0)
        columns = pl.ds(first, count)
        return [
            send(near.at[step, :, columns], part.at[step - 1, :, columns],
                 sends.at[stage, q, step - 1], recvs.at[stage, q, step - 1], along(a, step))
            for step in (1, 3, 2)
        ]

    home1 = first_back(6, pick1, bck1)

    for copies in final2:
        wait_all(copies)

    def backward(m, _):
        scaled = slot2[m].reshape(256, WIDTH)
        hidden_grad = dot(scaled, w_dn[...], (1, 1))
        here = pl.ds(pl.multiple_of(m * 256, 256), 256)
        projected = pre[here]
        pre_gate = projected[:, :HID]
        pre_up = projected[:, HID:]
        sigmoid_gate = jax.nn.sigmoid(pre_gate)
        grad_gate = hidden_grad * pre_up * sigmoid_gate * (1.0 + pre_gate * (1.0 - sigmoid_gate))
        grad_up = hidden_grad * (pre_gate * sigmoid_gate)
        both = jnp.concatenate([grad_gate, grad_up], axis=1).astype(BF)
        pre_grad[here] = both
        pick2[m] = dot(both, w_gu[...], (1, 1)).astype(BF).reshape(4, 4, 16, WIDTH)
        return 0

    lax.fori_loop(0, 4, backward, 0)
    home2 = first_back(7, pick2, bck2)

    turn1, turn2 = [], []
    for q in range(len(INBOUND)):
        wait_all(home1[q])
        turn1.append(second_back(8, q, bck1, back1))

    quarters = [
        pl.multiple_of(QUARTER * (2 * hi + c), QUARTER)
        for c in (1 - core, core)
        for hi in (1 - y_hi, y_hi)
    ]

    def gradients(first, from_core):
        def one(t, _):
            here = pl.ds(pl.multiple_of(first + t * 256, 256), 256)
            there = pl.ds(pl.multiple_of(t * 256, 256), 256)
            rows = slot1[:, :, :, :, here].reshape(1024, 256)
            result = dot(rows, pre_grad[...], (0, 0))
            if from_core is not None:
                result = result + core_gu[from_core, there].astype(F32)
            w_gu[here] = result.astype(BF)
            scaled = slot2[:, :, :, :, here].reshape(1024, 256)
            result = dot(hid[...], scaled, (0, 0))
            if from_core is not None:
                result = result + core_dn[from_core, :, there].astype(F32)
            w_dn[:, here] = result.astype(BF)
            return 0

        lax.fori_loop(0, 2, one, 0)

    to_core = []
    for j in range(2):
        gradients(quarters[j], None)
        part_of = pl.ds(quarters[j], QUARTER)
        to_core.append([
            send(w_gu.at[part_of], core_gu.at[j], grad_send.at[2 * j], grad_recv.at[2 * j], other_core),
            send(w_dn.at[:, part_of], core_dn.at[j], grad_send.at[2 * j + 1],
                 grad_recv.at[2 * j + 1], other_core),
        ])
    for q in range(len(INBOUND)):
        wait_all(home2[q])
        turn2.append(second_back(9, q, bck2, back2))

    wait_all(to_core[0])
    gradients(quarters[2], 0)
    across = []
    for p in range(2):
        across.append(send(
            w_gu.at[pl.ds(pl.multiple_of(quarters[2] + p * 256, 256), 256)],
            lane_gu.at[pl.ds(p * 256, 256)],
            grad_send.at[4 + p], grad_recv.at[4 + p], along(1, 2),
        ))
    across.append(send(
        w_dn.at[:, pl.ds(quarters[2], QUARTER)], lane_dn, grad_send.at[6], grad_recv.at[6], along(1, 2),
    ))
    wait_all(to_core[1])
    gradients(quarters[3], 1)

    last1, last2 = [], []
    for q in range(len(INBOUND)):
        wait_all(turn1[q])
        last1.append(combine(10, q, back1, gated, near1, part1))

    moves_own = moving[ex] == y_hi
    relocated, stayed = [], []
    for p in range(2):
        across[p].wait()
        mine = w_gu[pl.ds(pl.multiple_of(quarters[3] + p * 256, 256), 256)]
        theirs = lane_gu[pl.ds(p * 256, 256)]
        out_rows = pl.ds(pl.multiple_of(quarters[0] + p * 256, 256), 256)
        stay_rows = pl.ds(pl.multiple_of(quarters[1] + p * 256, 256), 256)
        w_gu[out_rows] = jnp.where(moves_own, mine, theirs)
        w_gu[stay_rows] = jnp.where(moves_own, theirs, mine)
        relocated.append(send(
            w_gu.at[out_rows], got_gu.at[pl.ds(p * 256, 256)],
            grad_send.at[7 + p], grad_recv.at[7 + p], along(0, 2),
        ))
        stayed.append(keep(w_gu.at[stay_rows], stay_gu.at[pl.ds(p * 256, 256)], out_sem.at[p]))
    across[2].wait()
    mine = w_dn[:, pl.ds(quarters[3], QUARTER)]
    theirs = lane_dn[...]
    w_dn[:, pl.ds(quarters[0], QUARTER)] = jnp.where(moves_own, mine, theirs)
    w_dn[:, pl.ds(quarters[1], QUARTER)] = jnp.where(moves_own, theirs, mine)
    relocated.append(send(
        w_dn.at[:, pl.ds(quarters[0], QUARTER)], got_dn, grad_send.at[9], grad_recv.at[9], along(0, 2),
    ))
    stayed.append(keep(w_dn.at[:, pl.ds(quarters[1], QUARTER)], stay_dn, out_sem.at[2]))

    for q in range(len(INBOUND)):
        wait_all(turn2[q])
        last2.append(combine(11, q, back2, onehot, near2, part2))

    def total(copies, near, part, result):
        for q, (_, _, _, first, count) in enumerate(INBOUND):
            wait_all(copies[q])
            span = slice(first, first + count)
            summed = near[0, :, span].astype(F32)
            for step in range(3):
                summed = summed + part[step, :, span].astype(F32)
            result[:, span] = summed.astype(BF)

    total(last1, near1, part1, mixed)
    total(last2, near2, part2, token_grad)
    wait_all(stayed)
    wait_all(relocated)


def on_device(tokens, routes, gates, out_grad, expert_gate_up, expert_down, moving_slot):
    vmem, anywhere = pl.BlockSpec(memory_space=pltpu.VMEM), pl.BlockSpec(memory_space=pl.ANY)
    slots = (4, 4, 4, CAP, WIDTH)
    sds = jax.ShapeDtypeStruct
    dma = pltpu.SemaphoreType.DMA
    results = pl.pallas_call(
        kernel,
        out_shape=(
            sds((ROWS, WIDTH), BF), sds((ROWS, WIDTH), BF),
            sds((QUARTER, FULL), BF), sds((HID, QUARTER), BF),
            sds((QUARTER, FULL), BF), sds((HID, QUARTER), BF),
            sds(slots, BF), sds(slots, BF), sds(slots, BF), sds(slots, BF),
        ),
        in_specs=[pl.BlockSpec(memory_space=pltpu.SMEM), vmem, vmem, vmem, vmem, anywhere, anywhere],
        out_specs=(vmem, vmem) + (anywhere,) * 8,
        scratch_shapes=[
            pltpu.VMEM((4, ROWS, WIDTH), BF), pltpu.VMEM((4, ROWS, WIDTH), BF),
            pltpu.VMEM(slots, BF), pltpu.VMEM(slots, BF),
            pltpu.VMEM(slots, BF), pltpu.VMEM(slots, BF),
            pltpu.VMEM((WIDTH, FULL), BF), pltpu.VMEM((HID, WIDTH), BF),
            pltpu.VMEM((1024, FULL), F32), pltpu.VMEM((1024, HID), BF), pltpu.VMEM((1024, FULL), BF),
            pltpu.VMEM(slots, BF), pltpu.VMEM(slots, BF),
            pltpu.VMEM((3, ROWS, WIDTH), BF), pltpu.VMEM((3, ROWS, WIDTH), BF),
            pltpu.VMEM((2, QUARTER, FULL), BF), pltpu.VMEM((2, HID, QUARTER), BF),
            pltpu.VMEM((QUARTER, FULL), BF), pltpu.VMEM((HID, QUARTER), BF),
            pltpu.VMEM((3, 4, ROWS, 128), BF),
            pltpu.VMEM((3, 4, ROWS, 256), BF), pltpu.VMEM((3, 4, ROWS, 256), BF),
            dma((12, 3, 3)), dma((12, 3, 3)), dma((3, 3)), dma((3, 3)), dma((12, 3)), dma((2,)),
            dma((10,)), dma((10,)), dma((3,)),
        ],
        compiler_params=pltpu.CompilerParams(
            collective_id=0, has_side_effects=True, vmem_limit_bytes=64 * 2**20 - 2**16
        ),
        cost_estimate=pl.CostEstimate(flops=27 * 10**9, bytes_accessed=40 * 10**6, transcendentals=10**6),
    )(moving_slot, tokens, routes, gates, out_grad, expert_gate_up, expert_down)
    mixed, token_grad, stay_gu, stay_dn, got_gu, got_dn = results[:6]
    moved = jnp.arange(2, dtype=jnp.int32)[:, None, None] == moving_slot[lax.axis_index("expert")]
    gate_up_grad = jnp.where(moved, got_gu[None], stay_gu[None])
    down_grad = jnp.where(moved, got_dn[None], stay_dn[None])
    return mixed, token_grad, gate_up_grad, down_grad


def solution(mesh):
    rows, whole = P(("dp", "expert"), None), P("expert", None, None)
    return jax.shard_map(
        on_device,
        mesh=mesh,
        in_specs=(rows, rows, rows, rows, whole, whole, P()),
        out_specs=(rows, rows, P("expert", "dp", None), P("expert", None, "dp")),
        check_vma=False,
    )
```

```python
import jax
import jax.numpy as jnp
from jax import lax
from jax.experimental import pallas as pl
from jax.experimental.pallas import tpu as pltpu
from jax.sharding import PartitionSpec as P

MESH = pl.DeviceIdType.MESH
BF, F32 = jnp.bfloat16, jnp.float32

ROWS, WIDTH, HID, TOP, CAP = 128, 2048, 704, 6, 16
FULL = 2 * HID
QUARTER = WIDTH // 4

OUTBOUND = (
    ((0, 1, 2, 0, 640), (1, 2, 0, 640, 640), (2, 0, 1, 1280, 768)),
    ((0, 1, 2, 0, 768), (1, 2, 0, 768, 640), (2, 0, 1, 1408, 640)),
)
INBOUND = ((0, 1, 2, 0, 768), (1, 2, 0, 768, 768), (2, 0, 1, 1536, 512))

SCHEDULE = (
    "rows_home", "turn1", "to_core", "to_core", "kept0", "across", "across", "across", "kept1",
    "turn2", "finish1", "relocate", "across", "relocate", "across", "relocate", "across",
    "finish2", "relocate", "relocate", "relocate",
)
MASKS = len({chunk[:3] for chunk in OUTBOUND[0] + OUTBOUND[1] + INBOUND})


def device_at(x, y, z, core):
    return ((y // 2) * 2 + core, x * 8 + (y % 2) * 4 + z)


def dot(a, b, contract):
    return lax.dot_general(a, b, ((contract[:1], contract[1:]), ((), ())), preferred_element_type=F32)


def kernel(
    moving, tokens, routes, gates, out_grad, gate_up, down,
    mixed, token_grad, stay_gu, stay_dn, got_gu, got_dn, fwd1, fwd2, bck1, bck2,
    near1, near2, pick1, pick2, slot1, slot2, w_gu, w_dn, hid, pre_grad,
    back1, back2, part1, part2, core_gu, core_dn, lane_gu, lane_dn, g_gu, info, gated,
    sends, recvs, info_send, info_recv, local_sem, w_sem, grad_send, grad_recv, out_sem,
):
    dp, ex = lax.axis_index("dp"), lax.axis_index("expert")
    y_hi, core = dp // 2, dp % 2
    me = (ex // 8, y_hi * 2 + (ex // 4) % 2, ex % 4)

    def along(axis, step):
        place = list(me)
        place[axis] = (place[axis] + step) % 4
        return device_at(*place, core)

    other_core = device_at(*me, 1 - core)

    barrier = pltpu.get_barrier_semaphore()
    for axis in range(3):
        for step in (1, 2, 3):
            pl.semaphore_signal(barrier, inc=1, device_id=along(axis, step), device_id_type=MESH)
    pl.semaphore_signal(barrier, inc=1, device_id=other_core, device_id_type=MESH)

    load_gu = pltpu.make_async_copy(gate_up.at[y_hi], w_gu, w_sem.at[0])
    load_dn = pltpu.make_async_copy(down.at[y_hi], w_dn, w_sem.at[1])
    load_gu.start()
    load_dn.start()
    pl.semaphore_wait(barrier, 10)

    def send(src, dst, send_sem, recv_sem, device):
        copy = pltpu.make_async_remote_copy(
            src_ref=src, dst_ref=dst, send_sem=send_sem, recv_sem=recv_sem,
            device_id=device, device_id_type=MESH,
        )
        copy.start()
        return copy

    def keep(src, dst, sem):
        copy = pltpu.make_async_copy(src, dst, sem)
        copy.start()
        return copy

    def wait_all(copies):
        for copy in copies:
            copy.wait()

    def fixed(axis, index, ref, columns):
        spot = [slice(None)] * 3
        spot[axis] = index
        return ref.at[(*spot, slice(None), columns)]

    def gather_axis(stage, source, near):
        started = []
        for q, (a, _, _, first, count) in enumerate(OUTBOUND[stage % 2]):
            columns = pl.ds(first, count)
            started.append([
                send(source.at[:, columns], near.at[step, :, columns],
                     sends.at[stage, q, step - 1], recvs.at[stage, q, step - 1], along(a, step))
                for step in (1, 3, 2)
            ])
        return started

    own_rows = [keep(tokens, near1.at[0], out_sem.at[6]), keep(out_grad, near2.at[0], out_sem.at[7])]

    line = lax.broadcasted_iota(jnp.int32, (128, ROWS), 0)
    name = line % 64
    hits = jnp.zeros((128, ROWS), F32)
    weight = jnp.zeros((128, ROWS), F32)
    all_routes, all_gates = routes[...], gates[...].astype(F32)
    for k in range(TOP):
        same = all_routes[k : k + 1] == name
        hits = hits + jnp.where(same, 1.0, 0.0)
        weight = weight + jnp.where(same, all_gates[k : k + 1], 0.0)
    earlier = lax.broadcasted_iota(jnp.int32, (ROWS, ROWS), 0) < lax.broadcasted_iota(
        jnp.int32, (ROWS, ROWS), 1
    )
    rank = dot(hits.astype(BF), jnp.where(earlier, 1.0, 0.0).astype(BF), (1, 0))
    own_info = jnp.where(line < 64, jnp.where(hits > 0.5, rank, 99.0), weight).astype(BF)
    for axis in range(3):
        info[axis, 0] = own_info
    info_copies = [
        [
            send(info.at[axis, 0], info.at[axis, step],
                 info_send.at[axis, step - 1], info_recv.at[axis, step - 1], along(axis, step))
            for step in (1, 3, 2)
        ]
        for axis in range(3)
    ]
    gather1 = gather_axis(0, tokens, near1)
    wait_all(own_rows)

    def pick_masks(number_of, axis, b, c):
        row = lax.broadcasted_iota(jnp.int32, (128, 256), 0)
        column = lax.broadcasted_iota(jnp.int32, (128, 256), 1)
        place = [None, None, None]
        place[axis], place[b], place[c] = me[axis], column // 64, (column // 16) % 4
        expert = 2 * (place[0] * 8 + (place[1] % 2) * 4 + place[2]) + place[1] // 2
        choose_rank = jnp.where(row == expert, 1.0, 0.0).astype(BF)
        choose_gate = jnp.where(row == expert + 64, 1.0, 0.0).astype(BF)
        number = (lax.broadcasted_iota(jnp.int32, (ROWS, 256), 1) % 16).astype(F32)

        def one(step, _):
            ranks = dot(info[axis, step], choose_rank, (0, 0))
            scale = dot(info[axis, step], choose_gate, (0, 0))
            live = ranks == number
            gated[number_of, step] = jnp.where(live, scale, 0.0).astype(BF)
            return 0

        lax.fori_loop(0, 4, one, 0)

    def mask_of(which, step, with_gate):
        mask = gated[which, step]
        return mask if with_gate else jnp.where(mask.astype(F32) != 0.0, 1.0, 0.0).astype(BF)

    def pick(chunk, near, with_gate, picked):
        a, b, c, first, count = chunk
        which = masks[a, b, c]

        def one(step, _):
            rows = dot(mask_of(which, step, with_gate), near[step, :, first : first + count], (0, 0))
            source = (me[a] - step + 4) % 4
            picked[:, :, source, :, first : first + count] = rows.astype(BF).reshape(4, 4, 16, count)
            return 0

        lax.fori_loop(0, 4, one, 0)

    def second_axis(stage, q, picked, onward):
        a, b, _, first, count = OUTBOUND[stage % 2][q]
        columns = pl.ds(first, count)
        landing = (
            onward.at[:, :, me[b], :, columns] if a < b else onward.at[:, me[b], :, :, columns]
        )
        copies = [
            send(picked.at[(me[b] + step) % 4, :, :, :, columns], landing,
                 sends.at[stage, q, step - 1], recvs.at[stage, q, step - 1], along(b, step))
            for step in (1, 3, 2)
        ]
        copies.append(keep(picked.at[me[b], :, :, :, columns], landing, local_sem.at[stage, q]))
        return copies

    def third_axis(stage, q, onward, slots):
        _, _, c, first, count = OUTBOUND[stage % 2][q]
        columns = pl.ds(first, count)
        landing = fixed(c, me[c], slots, columns)
        copies = [
            send(onward.at[(me[c] + step) % 4, :, :, :, columns], landing,
                 sends.at[stage, q, step - 1], recvs.at[stage, q, step - 1], along(c, step))
            for step in (1, 3, 2)
        ]
        copies.append(keep(onward.at[me[c], :, :, :, columns], landing, local_sem.at[stage, q]))
        return copies

    spread1, spread2, final1, final2 = [], [], [], []
    for copies in info_copies:
        wait_all(copies)
    masks = {}
    for axis, b, c in sorted({chunk[:3] for chunk in OUTBOUND[0] + OUTBOUND[1] + INBOUND}):
        masks[axis, b, c] = len(masks)
        pick_masks(masks[axis, b, c], axis, b, c)
    gather2 = gather_axis(1, out_grad, near2)
    for q, chunk in enumerate(OUTBOUND[0]):
        wait_all(gather1[q])
        pick(chunk, near1, False, pick1)
        spread1.append(second_axis(2, q, pick1, fwd1))
    for q, chunk in enumerate(OUTBOUND[1]):
        wait_all(gather2[q])
        pick(chunk, near2, True, pick2)
        spread2.append(second_axis(3, q, pick2, fwd2))
    for q in range(len(OUTBOUND[0])):
        wait_all(spread1[q])
        final1.append(third_axis(4, q, fwd1, slot1))
    for q in range(len(OUTBOUND[1])):
        wait_all(spread2[q])
        final2.append(third_axis(5, q, fwd2, slot2))

    load_gu.wait()
    load_dn.wait()
    for copies in final1:
        wait_all(copies)

    def forward(m, _):
        rows = slot1[m].reshape(256, WIDTH)
        projected = dot(rows, w_gu[...], (1, 0))
        here = pl.ds(pl.multiple_of(m * 256, 256), 256)
        pre_gate = projected[:, :HID]
        pre_up = projected[:, HID:]
        sigmoid_gate = jax.nn.sigmoid(pre_gate)
        activated = pre_gate * sigmoid_gate
        hidden = (activated * pre_up).astype(BF)
        hid[here] = hidden
        by_gate = pre_up * sigmoid_gate * (1.0 + pre_gate * (1.0 - sigmoid_gate))
        pre_grad[here] = jnp.concatenate([by_gate, activated], axis=1).astype(BF)
        pick1[m] = dot(hidden, w_dn[...], (1, 0)).astype(BF).reshape(4, 4, 16, WIDTH)
        return 0

    lax.fori_loop(0, 4, forward, 0)

    def first_back(stage, result, onward):
        started = []
        for q, (_, _, c, first, count) in enumerate(INBOUND):
            columns = pl.ds(first, count)
            landing = onward.at[me[c], :, :, :, columns]
            copies = [
                send(fixed(c, (me[c] + step) % 4, result, columns), landing,
                     sends.at[stage, q, step - 1], recvs.at[stage, q, step - 1], along(c, step))
                for step in (1, 3, 2)
            ]
            copies.append(keep(fixed(c, me[c], result, columns), landing, local_sem.at[stage, q]))
            started.append(copies)
        return started

    def second_back(stage, q, onward, back):
        a, b, _, first, count = INBOUND[q]
        columns = pl.ds(first, count)

        def to(index):
            return onward.at[:, :, index, :, columns] if a < b else onward.at[:, index, :, :, columns]

        landing = back.at[me[b], :, :, :, columns]
        copies = [
            send(to((me[b] + step) % 4), landing,
                 sends.at[stage, q, step - 1], recvs.at[stage, q, step - 1], along(b, step))
            for step in (1, 3, 2)
        ]
        copies.append(keep(to(me[b]), landing, local_sem.at[stage, q]))
        return copies

    def combine(stage, q, back, with_gate, near, part):
        a, b, c, first, count = INBOUND[q]
        which = masks[a, b, c]

        def one(step, _):
            target = (me[a] + step) % 4
            rows = back[:, :, target, :, first : first + count].reshape(256, count)
            near[step, :, first : first + count] = dot(
                mask_of(which, (4 - step) % 4, with_gate), rows, (1, 0)
            ).astype(BF)
            return 0

        lax.fori_loop(0, 4, one, 0)
        columns = pl.ds(first, count)
        return [
            send(near.at[step, :, columns], part.at[step - 1, :, columns],
                 sends.at[stage, q, step - 1], recvs.at[stage, q, step - 1], along(a, step))
            for step in (1, 3, 2)
        ]

    home1 = first_back(6, pick1, bck1)

    for copies in final2:
        wait_all(copies)

    def backward(m, _):
        scaled = slot2[m].reshape(256, WIDTH)
        hidden_grad = dot(scaled, w_dn[...], (1, 1))
        here = pl.ds(pl.multiple_of(m * 256, 256), 256)
        twice = jnp.concatenate([hidden_grad, hidden_grad], axis=1)
        pre_grad[here] = (twice * pre_grad[here].astype(F32)).astype(BF)
        return 0

    def row_gradient(m, _):
        here = pl.ds(pl.multiple_of(m * 256, 256), 256)
        pick2[m] = dot(pre_grad[here], w_gu[...], (1, 1)).astype(BF).reshape(4, 4, 16, WIDTH)
        return 0

    lax.fori_loop(0, 4, backward, 0)

    quarters = [
        pl.multiple_of(QUARTER * (2 * hi + c), QUARTER)
        for c in (1 - core, core)
        for hi in (1 - y_hi, y_hi)
    ]

    def grad_gu(first, t, from_core, w_next):
        here = pl.ds(pl.multiple_of(first + t * 256, 256), 256)
        there = pl.ds(pl.multiple_of(t * 256, 256), 256)
        rows = slot1[:, :, :, :, here].reshape(1024, 256)
        result = dot(rows, pre_grad[...], (0, 0))
        if from_core is not None:
            result = result + core_gu[from_core, there].astype(F32)
        w_next[here] = result.astype(BF)

    def grad_dn(first, t, from_core, w_next):
        here = pl.ds(pl.multiple_of(first + t * 256, 256), 256)
        there = pl.ds(pl.multiple_of(t * 256, 256), 256)
        scaled = slot2[:, :, :, :, here].reshape(1024, 256)
        result = dot(hid[...], scaled, (0, 0))
        if from_core is not None:
            result = result + core_dn[from_core, :, there].astype(F32)
        w_next[:, here] = result.astype(BF)

    def gradients(first, from_core, w_gu_next, w_dn_next):
        def one(t, _):
            grad_gu(first, t, from_core, w_gu_next)
            grad_dn(first, t, from_core, w_dn_next)
            return 0

        lax.fori_loop(0, 2, one, 0)

    pieces = (("gu", 0, 128), ("gu", 128, 128), ("dn", 0, 256), ("gu", 256, 128), ("gu", 384, 128), ("dn", 256, 256))

    def piece_of(p, quarter, mine):
        kind, first, size = pieces[p]
        if kind == "gu":
            return (g_gu if mine else lane_gu), (pl.ds(pl.multiple_of(quarter + first, 128), size),)
        return (w_dn if mine else lane_dn), (slice(None), pl.ds(pl.multiple_of(quarter + first, 128), size))

    across, relocated, stayed = [], [], []

    def send_across(p):
        source, span = piece_of(p, quarters[2], True)
        target, there = piece_of(p, 0, False)
        across.append(send(
            source.at[span], target.at[there], grad_send.at[4 + p], grad_recv.at[4 + p], along(1, 2),
        ))

    moves_own = moving[ex] == y_hi

    def relocate(p):
        across[p].wait()
        held, span = piece_of(p, quarters[3], True)
        lane_held, there = piece_of(p, 0, False)
        mine, theirs = held[span], lane_held[there]
        out_span, stay_span = piece_of(p, quarters[0], True)[1], piece_of(p, quarters[1], True)[1]
        held[out_span] = jnp.where(moves_own, mine, theirs)
        held[stay_span] = jnp.where(moves_own, theirs, mine)
        got, stay = (got_gu, stay_gu) if pieces[p][0] == "gu" else (got_dn, stay_dn)
        relocated.append(send(
            held.at[out_span], got.at[there], grad_send.at[10 + p], grad_recv.at[10 + p], along(0, 2),
        ))
        stayed.append(keep(held.at[stay_span], stay.at[there], out_sem.at[p]))

    to_core, home2, turn1, turn2, last1, last2 = [], [], [], [], [], []

    def gradients_to_core():
        j = len(to_core)
        gradients(quarters[j], None, g_gu, w_dn)
        part_of = pl.ds(quarters[j], QUARTER)
        to_core.append([
            send(g_gu.at[part_of], core_gu.at[j], grad_send.at[2 * j], grad_recv.at[2 * j], other_core),
            send(w_dn.at[:, part_of], core_dn.at[j], grad_send.at[2 * j + 1],
                 grad_recv.at[2 * j + 1], other_core),
        ])

    def gradients_kept(j):
        wait_all(to_core[j])
        gradients(quarters[2 + j], j, g_gu, w_dn)

    def rows_home():
        lax.fori_loop(0, 4, row_gradient, 0)
        home2.extend(first_back(7, pick2, bck2))

    def turn(stage, home, onward, back, turned):
        for q in range(len(INBOUND)):
            wait_all(home[q])
            turned.append(second_back(stage, q, onward, back))

    def finish(stage, turned, back, with_gate, near, part, last):
        for q in range(len(INBOUND)):
            wait_all(turned[q])
            last.append(combine(stage, q, back, with_gate, near, part))

    steps = {
        "rows_home": rows_home,
        "turn1": lambda: turn(8, home1, bck1, back1, turn1),
        "turn2": lambda: turn(9, home2, bck2, back2, turn2),
        "finish1": lambda: finish(10, turn1, back1, True, near1, part1, last1),
        "finish2": lambda: finish(11, turn2, back2, False, near2, part2, last2),
        "to_core": gradients_to_core,
        "kept0": lambda: gradients_kept(0),
        "kept1": lambda: gradients_kept(1),
        "across": lambda: send_across(len(across)),
        "relocate": lambda: relocate(len(relocated)),
    }
    for step in SCHEDULE:
        steps[step]()

    def total(copies, near, part, result, sem):
        for q, (_, _, _, first, count) in enumerate(INBOUND):
            wait_all(copies[q])
            span = slice(first, first + count)
            summed = near[0, :, span].astype(F32)
            for step in range(3):
                summed = summed + part[step, :, span].astype(F32)
            near[0, :, span] = summed.astype(BF)
        return keep(near.at[0], result, out_sem.at[sem])

    stayed.append(total(last1, near1, part1, mixed, 8))
    stayed.append(total(last2, near2, part2, token_grad, 9))
    wait_all(stayed)
    wait_all(relocated)


def place(moving, mixed, token_grad, stay_gu, stay_dn, got_gu, got_dn,
          mixed_out, token_grad_out, gu_out, dn_out, rows_held, gu_held, dn_held, sem_in, sem_out):
    moved = moving[lax.axis_index("expert")]
    moves = [
        (mixed, rows_held.at[0], mixed_out), (token_grad, rows_held.at[1], token_grad_out),
    ]
    for i, (slot, gu, dn) in enumerate(((moved, got_gu, got_dn), (1 - moved, stay_gu, stay_dn))):
        for p in range(2):
            rows = pl.ds(p * 256, 256)
            moves.append((gu.at[rows], gu_held.at[i, rows], gu_out.at[slot, rows]))
        moves.append((dn, dn_held.at[i], dn_out.at[slot]))
    loads = [pltpu.make_async_copy(src, held, sem_in.at[i]) for i, (src, held, _) in enumerate(moves)]
    stores = [pltpu.make_async_copy(held, dst, sem_out.at[i]) for i, (_, held, dst) in enumerate(moves)]
    for copy in loads:
        copy.start()
    for load, store in zip(loads, stores):
        load.wait()
        store.start()
    for copy in stores:
        copy.wait()


def on_device(tokens, routes, gates, out_grad, expert_gate_up, expert_down, moving_slot):
    vmem, anywhere = pl.BlockSpec(memory_space=pltpu.VMEM), pl.BlockSpec(memory_space=pl.ANY)
    slots = (4, 4, 4, CAP, WIDTH)
    sds = jax.ShapeDtypeStruct
    dma = pltpu.SemaphoreType.DMA
    results = pl.pallas_call(
        kernel,
        out_shape=(
            sds((ROWS, WIDTH), BF), sds((ROWS, WIDTH), BF),
            sds((QUARTER, FULL), BF), sds((HID, QUARTER), BF),
            sds((QUARTER, FULL), BF), sds((HID, QUARTER), BF),
            sds(slots, BF), sds(slots, BF), sds(slots, BF), sds(slots, BF),
        ),
        in_specs=[pl.BlockSpec(memory_space=pltpu.SMEM), anywhere, vmem, vmem] + [anywhere] * 3,
        out_specs=(anywhere,) * 10,
        scratch_shapes=[
            pltpu.VMEM((4, ROWS, WIDTH), BF), pltpu.VMEM((4, ROWS, WIDTH), BF),
            pltpu.VMEM(slots, BF), pltpu.VMEM(slots, BF),
            pltpu.VMEM(slots, BF), pltpu.VMEM(slots, BF),
            pltpu.VMEM((WIDTH, FULL), BF), pltpu.VMEM((HID, WIDTH), BF),
            pltpu.VMEM((1024, HID), BF), pltpu.VMEM((1024, FULL), BF),
            pltpu.VMEM(slots, BF), pltpu.VMEM(slots, BF),
            pltpu.VMEM((3, ROWS, WIDTH), BF), pltpu.VMEM((3, ROWS, WIDTH), BF),
            pltpu.VMEM((2, QUARTER, FULL), BF), pltpu.VMEM((2, HID, QUARTER), BF),
            pltpu.VMEM((QUARTER, FULL), BF), pltpu.VMEM((HID, QUARTER), BF),
            pltpu.VMEM((WIDTH, FULL), BF),
            pltpu.VMEM((3, 4, ROWS, 128), BF),
            pltpu.VMEM((MASKS, 4, ROWS, 256), BF),
            dma((12, 6, 3)), dma((12, 6, 3)), dma((3, 3)), dma((3, 3)), dma((12, 6)), dma((2,)),
            dma((16,)), dma((16,)), dma((10,)),
        ],
        compiler_params=pltpu.CompilerParams(
            collective_id=0, has_side_effects=True, vmem_limit_bytes=64 * 2**20 - 2**16
        ),
        cost_estimate=pl.CostEstimate(flops=27 * 10**9, bytes_accessed=40 * 10**6, transcendentals=10**6),
    )(moving_slot, tokens, routes.T, gates.T, out_grad, expert_gate_up, expert_down)
    return pl.pallas_call(
        place,
        out_shape=(
            sds((ROWS, WIDTH), BF), sds((ROWS, WIDTH), BF),
            sds((2, QUARTER, FULL), BF), sds((2, HID, QUARTER), BF),
        ),
        in_specs=[pl.BlockSpec(memory_space=pltpu.SMEM)] + [anywhere] * 6,
        out_specs=(anywhere,) * 4,
        scratch_shapes=[
            pltpu.VMEM((2, ROWS, WIDTH), BF), pltpu.VMEM((2, QUARTER, FULL), BF),
            pltpu.VMEM((2, HID, QUARTER), BF), dma((8,)), dma((8,)),
        ],
    )(moving_slot, *results[:6])


def solution(mesh):
    rows, whole = P(("dp", "expert"), None), P("expert", None, None)
    return jax.shard_map(
        on_device,
        mesh=mesh,
        in_specs=(rows, rows, rows, rows, whole, whole, P()),
        out_specs=(rows, rows, P("expert", "dp", None), P("expert", None, "dp")),
        check_vma=False,
    )
```

```python
import jax
import jax.numpy as jnp
from jax import lax
from jax.experimental import pallas as pl
from jax.experimental.pallas import tpu as pltpu
from jax.sharding import PartitionSpec as P

MESH = pl.DeviceIdType.MESH
BF, F32 = jnp.bfloat16, jnp.float32

ROWS, WIDTH, HID, TOP, CAP = 128, 2048, 704, 6, 16
FULL = 2 * HID
QUARTER = WIDTH // 4

OUTBOUND = (
    ((0, 1, 2, 0, 640), (1, 2, 0, 640, 640), (2, 0, 1, 1280, 768)),
    ((0, 1, 2, 0, 768), (1, 2, 0, 768, 640), (2, 0, 1, 1408, 640)),
)
INBOUND = ((0, 1, 2, 0, 640), (1, 2, 0, 640, 896), (2, 0, 1, 1536, 512))

SCHEDULE = (
    "rows_home", "turn1", "to_core", "to_core", "kept0", "across", "across", "across", "kept1",
    "turn2", "finish1", "relocate", "across", "relocate", "across", "relocate", "across",
    "finish2", "relocate", "relocate", "relocate",
)
MASKS = len({chunk[:3] for chunk in OUTBOUND[0] + OUTBOUND[1] + INBOUND})


def device_at(x, y, z, core):
    return ((y // 2) * 2 + core, x * 8 + (y % 2) * 4 + z)


def dot(a, b, contract):
    return lax.dot_general(a, b, ((contract[:1], contract[1:]), ((), ())), preferred_element_type=F32)


def kernel(
    moving, tokens, routes, gates, out_grad, gate_up, down,
    mixed, token_grad, stay_gu, stay_dn, got_gu, got_dn, fwd1, fwd2, bck1, bck2,
    near1, near2, pick1, pick2, slot1, slot2, w_gu, w_dn, hid, pre_grad,
    back1, back2, part1, part2, core_gu, core_dn, lane_gu, lane_dn, g_gu, info, gated,
    sends, recvs, info_send, info_recv, w_sem, grad_send, grad_recv, out_sem,
):
    dp, ex = lax.axis_index("dp"), lax.axis_index("expert")
    y_hi, core = dp // 2, dp % 2
    me = (ex // 8, y_hi * 2 + (ex // 4) % 2, ex % 4)

    def along(axis, step):
        place = list(me)
        place[axis] = (place[axis] + step) % 4
        return device_at(*place, core)

    other_core = device_at(*me, 1 - core)

    barrier = pltpu.get_barrier_semaphore()
    for axis in range(3):
        for step in (1, 2, 3):
            pl.semaphore_signal(barrier, inc=1, device_id=along(axis, step), device_id_type=MESH)
    pl.semaphore_signal(barrier, inc=1, device_id=other_core, device_id_type=MESH)

    load_gu = pltpu.make_async_copy(gate_up.at[y_hi], w_gu, w_sem.at[0])
    load_dn = pltpu.make_async_copy(down.at[y_hi], w_dn, w_sem.at[1])
    load_gu.start()
    load_dn.start()
    pl.semaphore_wait(barrier, 10)

    def send(src, dst, send_sem, recv_sem, device):
        copy = pltpu.make_async_remote_copy(
            src_ref=src, dst_ref=dst, send_sem=send_sem, recv_sem=recv_sem,
            device_id=device, device_id_type=MESH,
        )
        copy.start()
        return copy

    def keep(src, dst, sem):
        copy = pltpu.make_async_copy(src, dst, sem)
        copy.start()
        return copy

    def wait_all(copies):
        for copy in copies:
            copy.wait()

    def group(sent, received, send_sem, recv_sem):
        return [
            pltpu.make_async_copy(received, received, recv_sem),
            pltpu.make_async_copy(sent, sent, send_sem),
        ]

    def fixed(axis, index, ref, columns):
        spot = [slice(None)] * 3
        spot[axis] = index
        return ref.at[(*spot, slice(None), columns)]

    def gather_axis(stage, source, near):
        started = []
        for q, (a, _, _, first, count) in enumerate(OUTBOUND[stage % 2]):
            columns = pl.ds(first, count)
            sems = sends.at[stage, q], recvs.at[stage, q]
            for step in (1, 3, 2):
                send(source.at[:, columns], near.at[step, :, columns], *sems, along(a, step))
            whole = near.at[pl.ds(1, 3), :, columns]
            started.append(group(whole, whole, *sems))
        return started

    own_rows = [keep(tokens, near1.at[0], out_sem.at[6]), keep(out_grad, near2.at[0], out_sem.at[7])]

    line = lax.broadcasted_iota(jnp.int32, (128, ROWS), 0)
    name = line % 64
    hits = jnp.zeros((128, ROWS), F32)
    weight = jnp.zeros((128, ROWS), F32)
    all_routes, all_gates = routes[...], gates[...].astype(F32)
    for k in range(TOP):
        same = all_routes[k : k + 1] == name
        hits = hits + jnp.where(same, 1.0, 0.0)
        weight = weight + jnp.where(same, all_gates[k : k + 1], 0.0)
    earlier = lax.broadcasted_iota(jnp.int32, (ROWS, ROWS), 0) < lax.broadcasted_iota(
        jnp.int32, (ROWS, ROWS), 1
    )
    rank = dot(hits.astype(BF), jnp.where(earlier, 1.0, 0.0).astype(BF), (1, 0))
    own_info = jnp.where(line < 64, jnp.where(hits > 0.5, rank, 99.0), weight).astype(BF)
    for axis in range(3):
        info[axis, 0] = own_info
    info_copies = []
    for axis in range(3):
        sems = info_send.at[axis], info_recv.at[axis]
        for step in (1, 3, 2):
            send(info.at[axis, 0], info.at[axis, step], *sems, along(axis, step))
        whole = info.at[axis, pl.ds(1, 3)]
        info_copies.append(group(whole, whole, *sems))
    gather1 = gather_axis(0, tokens, near1)
    wait_all(own_rows)

    def pick_masks(number_of, axis, b, c):
        row = lax.broadcasted_iota(jnp.int32, (128, 256), 0)
        column = lax.broadcasted_iota(jnp.int32, (128, 256), 1)
        place = [None, None, None]
        place[axis], place[b], place[c] = me[axis], column // 64, (column // 16) % 4
        expert = 2 * (place[0] * 8 + (place[1] % 2) * 4 + place[2]) + place[1] // 2
        choose_rank = jnp.where(row == expert, 1.0, 0.0).astype(BF)
        choose_gate = jnp.where(row == expert + 64, 1.0, 0.0).astype(BF)
        number = (lax.broadcasted_iota(jnp.int32, (ROWS, 256), 1) % 16).astype(F32)

        def one(step, _):
            ranks = dot(info[axis, step], choose_rank, (0, 0))
            scale = dot(info[axis, step], choose_gate, (0, 0))
            live = ranks == number
            gated[number_of, step] = jnp.where(live, scale, 0.0).astype(BF)
            return 0

        lax.fori_loop(0, 4, one, 0)

    def mask_of(which, step, with_gate):
        mask = gated[which, step]
        return mask if with_gate else jnp.where(mask.astype(F32) != 0.0, 1.0, 0.0).astype(BF)

    def pick(chunk, near, with_gate, picked):
        a, b, c, first, count = chunk
        which = masks[a, b, c]

        def one(step, _):
            rows = dot(mask_of(which, step, with_gate), near[step, :, first : first + count], (0, 0))
            source = (me[a] - step + 4) % 4
            picked[:, :, source, :, first : first + count] = rows.astype(BF).reshape(4, 4, 16, count)
            return 0

        lax.fori_loop(0, 4, one, 0)

    def quarters_of(buffer, columns, sems):
        return group(
            buffer.at[pl.ds(0, 3), :, :, :, columns], buffer.at[:, :, :, :, columns], *sems
        )

    def second_axis(stage, q, picked, onward):
        a, b, _, first, count = OUTBOUND[stage % 2][q]
        columns = pl.ds(first, count)
        landing = (
            onward.at[:, :, me[b], :, columns] if a < b else onward.at[:, me[b], :, :, columns]
        )
        sems = sends.at[stage, q], recvs.at[stage, q]
        for step in (1, 3, 2):
            send(picked.at[(me[b] + step) % 4, :, :, :, columns], landing, *sems, along(b, step))
        keep(picked.at[me[b], :, :, :, columns], landing, sems[1])
        return quarters_of(onward, columns, sems)

    def third_axis(stage, q, onward, slots):
        _, _, c, first, count = OUTBOUND[stage % 2][q]
        columns = pl.ds(first, count)
        landing = fixed(c, me[c], slots, columns)
        sems = sends.at[stage, q], recvs.at[stage, q]
        for step in (1, 3, 2):
            send(onward.at[(me[c] + step) % 4, :, :, :, columns], landing, *sems, along(c, step))
        keep(onward.at[me[c], :, :, :, columns], landing, sems[1])
        return quarters_of(slots, columns, sems)

    spread1, spread2, final1, final2 = [], [], [], []
    for copies in info_copies:
        wait_all(copies)
    masks = {}
    for axis, b, c in sorted({chunk[:3] for chunk in OUTBOUND[0] + OUTBOUND[1] + INBOUND}):
        masks[axis, b, c] = len(masks)
        pick_masks(masks[axis, b, c], axis, b, c)
    gather2 = gather_axis(1, out_grad, near2)
    for q, chunk in enumerate(OUTBOUND[0]):
        wait_all(gather1[q])
        pick(chunk, near1, False, pick1)
        spread1.append(second_axis(2, q, pick1, fwd1))
    for q, chunk in enumerate(OUTBOUND[1]):
        wait_all(gather2[q])
        pick(chunk, near2, True, pick2)
        spread2.append(second_axis(3, q, pick2, fwd2))
    for q in range(len(OUTBOUND[0])):
        wait_all(spread1[q])
        final1.append(third_axis(4, q, fwd1, slot1))
    for q in range(len(OUTBOUND[1])):
        wait_all(spread2[q])
        final2.append(third_axis(5, q, fwd2, slot2))

    load_gu.wait()
    load_dn.wait()
    for copies in final1:
        wait_all(copies)

    def forward(m, _):
        rows = slot1[m].reshape(256, WIDTH)
        projected = dot(rows, w_gu[...], (1, 0))
        here = pl.ds(pl.multiple_of(m * 256, 256), 256)
        pre_gate = projected[:, :HID]
        pre_up = projected[:, HID:]
        sigmoid_gate = jax.nn.sigmoid(pre_gate)
        activated = pre_gate * sigmoid_gate
        hidden = (activated * pre_up).astype(BF)
        hid[here] = hidden
        by_gate = pre_up * sigmoid_gate * (1.0 + pre_gate * (1.0 - sigmoid_gate))
        pre_grad[here] = jnp.concatenate([by_gate, activated], axis=1).astype(BF)
        pick1[m] = dot(hidden, w_dn[...], (1, 0)).astype(BF).reshape(4, 4, 16, WIDTH)
        return 0

    lax.fori_loop(0, 4, forward, 0)

    def first_back(stage, result, onward):
        started = []
        for q, (_, _, c, first, count) in enumerate(INBOUND):
            columns = pl.ds(first, count)
            landing = onward.at[me[c], :, :, :, columns]
            sems = sends.at[stage, q], recvs.at[stage, q]
            for step in (1, 3, 2):
                send(fixed(c, (me[c] + step) % 4, result, columns), landing, *sems, along(c, step))
            keep(fixed(c, me[c], result, columns), landing, sems[1])
            started.append(quarters_of(onward, columns, sems))
        return started

    def second_back(stage, q, onward, back):
        a, b, _, first, count = INBOUND[q]
        columns = pl.ds(first, count)

        def to(index):
            return onward.at[:, :, index, :, columns] if a < b else onward.at[:, index, :, :, columns]

        landing = back.at[me[b], :, :, :, columns]
        sems = sends.at[stage, q], recvs.at[stage, q]
        for step in (1, 3, 2):
            send(to((me[b] + step) % 4), landing, *sems, along(b, step))
        keep(to(me[b]), landing, sems[1])
        return quarters_of(back, columns, sems)

    def combine(stage, q, back, with_gate, near, part):
        a, b, c, first, count = INBOUND[q]
        which = masks[a, b, c]

        def one(step, _):
            target = (me[a] + step) % 4
            rows = back[:, :, target, :, first : first + count].reshape(256, count)
            near[step, :, first : first + count] = dot(
                mask_of(which, (4 - step) % 4, with_gate), rows, (1, 0)
            ).astype(BF)
            return 0

        lax.fori_loop(0, 4, one, 0)
        columns = pl.ds(first, count)
        sems = sends.at[stage, q], recvs.at[stage, q]
        for step in (1, 3, 2):
            send(near.at[step, :, columns], part.at[step - 1, :, columns], *sems, along(a, step))
        whole = part.at[:, :, columns]
        return group(whole, whole, *sems)

    home1 = first_back(6, pick1, bck1)

    for copies in final2:
        wait_all(copies)

    def backward(m, _):
        scaled = slot2[m].reshape(256, WIDTH)
        hidden_grad = dot(scaled, w_dn[...], (1, 1))
        here = pl.ds(pl.multiple_of(m * 256, 256), 256)
        twice = jnp.concatenate([hidden_grad, hidden_grad], axis=1)
        pre_grad[here] = (twice * pre_grad[here].astype(F32)).astype(BF)
        return 0

    def row_gradient(m, _):
        here = pl.ds(pl.multiple_of(m * 256, 256), 256)
        pick2[m] = dot(pre_grad[here], w_gu[...], (1, 1)).astype(BF).reshape(4, 4, 16, WIDTH)
        return 0

    lax.fori_loop(0, 4, backward, 0)

    quarters = [
        pl.multiple_of(QUARTER * (2 * hi + c), QUARTER)
        for c in (1 - core, core)
        for hi in (1 - y_hi, y_hi)
    ]

    def grad_gu(first, t, from_core, w_next):
        here = pl.ds(pl.multiple_of(first + t * 256, 256), 256)
        there = pl.ds(pl.multiple_of(t * 256, 256), 256)
        rows = slot1[:, :, :, :, here].reshape(1024, 256)
        result = dot(rows, pre_grad[...], (0, 0))
        if from_core is not None:
            result = result + core_gu[from_core, there].astype(F32)
        w_next[here] = result.astype(BF)

    def grad_dn(first, t, from_core, w_next):
        here = pl.ds(pl.multiple_of(first + t * 256, 256), 256)
        there = pl.ds(pl.multiple_of(t * 256, 256), 256)
        scaled = slot2[:, :, :, :, here].reshape(1024, 256)
        result = dot(hid[...], scaled, (0, 0))
        if from_core is not None:
            result = result + core_dn[from_core, :, there].astype(F32)
        w_next[:, here] = result.astype(BF)

    def gradients(first, from_core, w_gu_next, w_dn_next):
        def one(t, _):
            grad_gu(first, t, from_core, w_gu_next)
            grad_dn(first, t, from_core, w_dn_next)
            return 0

        lax.fori_loop(0, 2, one, 0)

    pieces = (("gu", 0, 128), ("gu", 128, 128), ("dn", 0, 256), ("gu", 256, 128), ("gu", 384, 128), ("dn", 256, 256))

    def piece_of(p, quarter, mine):
        kind, first, size = pieces[p]
        if kind == "gu":
            return (g_gu if mine else lane_gu), (pl.ds(pl.multiple_of(quarter + first, 64), size),)
        return (w_dn if mine else lane_dn), (slice(None), pl.ds(pl.multiple_of(quarter + first, 128), size))

    across, relocated, stayed = [], [], []

    def send_across(p):
        source, span = piece_of(p, quarters[2], True)
        target, there = piece_of(p, 0, False)
        across.append(send(
            source.at[span], target.at[there], grad_send.at[4 + p], grad_recv.at[4 + p], along(1, 2),
        ))

    moves_own = moving[ex] == y_hi

    def relocate(p):
        across[p].wait()
        held, span = piece_of(p, quarters[3], True)
        lane_held, there = piece_of(p, 0, False)
        mine, theirs = held[span], lane_held[there]
        out_span, stay_span = piece_of(p, quarters[0], True)[1], piece_of(p, quarters[1], True)[1]
        held[out_span] = jnp.where(moves_own, mine, theirs)
        held[stay_span] = jnp.where(moves_own, theirs, mine)
        got, stay = (got_gu, stay_gu) if pieces[p][0] == "gu" else (got_dn, stay_dn)
        relocated.append(send(
            held.at[out_span], got.at[there], grad_send.at[10 + p], grad_recv.at[10 + p], along(0, 2),
        ))
        stayed.append(keep(held.at[stay_span], stay.at[there], out_sem.at[p]))

    to_core, home2, turn1, turn2, last1, last2 = [], [], [], [], [], []

    def gradients_to_core():
        j = len(to_core)
        gradients(quarters[j], None, g_gu, w_dn)
        part_of = pl.ds(quarters[j], QUARTER)
        to_core.append([
            send(g_gu.at[part_of], core_gu.at[j], grad_send.at[2 * j], grad_recv.at[2 * j], other_core),
            send(w_dn.at[:, part_of], core_dn.at[j], grad_send.at[2 * j + 1],
                 grad_recv.at[2 * j + 1], other_core),
        ])

    def gradients_kept(j):
        wait_all(to_core[j])
        gradients(quarters[2 + j], j, g_gu, w_dn)

    def rows_home():
        lax.fori_loop(0, 4, row_gradient, 0)
        home2.extend(first_back(7, pick2, bck2))

    def turn(stage, home, onward, back, turned):
        for q in range(len(INBOUND)):
            wait_all(home[q])
            turned.append(second_back(stage, q, onward, back))

    def finish(stage, turned, back, with_gate, near, part, last):
        for q in range(len(INBOUND)):
            wait_all(turned[q])
            last.append(combine(stage, q, back, with_gate, near, part))

    steps = {
        "rows_home": rows_home,
        "turn1": lambda: turn(8, home1, bck1, back1, turn1),
        "turn2": lambda: turn(9, home2, bck2, back2, turn2),
        "finish1": lambda: finish(10, turn1, back1, True, near1, part1, last1),
        "finish2": lambda: finish(11, turn2, back2, False, near2, part2, last2),
        "to_core": gradients_to_core,
        "kept0": lambda: gradients_kept(0),
        "kept1": lambda: gradients_kept(1),
        "across": lambda: send_across(len(across)),
        "relocate": lambda: relocate(len(relocated)),
    }
    for step in SCHEDULE:
        steps[step]()

    def total(copies, near, part, result, sem):
        for q, (_, _, _, first, count) in enumerate(INBOUND):
            wait_all(copies[q])
            span = slice(first, first + count)
            summed = near[0, :, span].astype(F32)
            for step in range(3):
                summed = summed + part[step, :, span].astype(F32)
            near[0, :, span] = summed.astype(BF)
        return keep(near.at[0], result, out_sem.at[sem])

    stayed.append(total(last1, near1, part1, mixed, 8))
    stayed.append(total(last2, near2, part2, token_grad, 9))
    wait_all(stayed)
    wait_all(relocated)


def place(moving, mixed, token_grad, stay_gu, stay_dn, got_gu, got_dn,
          mixed_out, token_grad_out, gu_out, dn_out, rows_held, gu_held, dn_held, sem_in, sem_out):
    moved = moving[lax.axis_index("expert")]
    moves = [
        (mixed, rows_held.at[0], mixed_out), (token_grad, rows_held.at[1], token_grad_out),
    ]
    for i, (slot, gu, dn) in enumerate(((moved, got_gu, got_dn), (1 - moved, stay_gu, stay_dn))):
        for p in range(2):
            rows = pl.ds(p * 256, 256)
            moves.append((gu.at[rows], gu_held.at[i, rows], gu_out.at[slot, rows]))
        moves.append((dn, dn_held.at[i], dn_out.at[slot]))
    loads = [pltpu.make_async_copy(src, held, sem_in.at[i]) for i, (src, held, _) in enumerate(moves)]
    stores = [pltpu.make_async_copy(held, dst, sem_out.at[i]) for i, (_, held, dst) in enumerate(moves)]
    for copy in loads:
        copy.start()
    for load, store in zip(loads, stores):
        load.wait()
        store.start()
    for copy in stores:
        copy.wait()


def on_device(tokens, routes, gates, out_grad, expert_gate_up, expert_down, moving_slot):
    vmem, anywhere = pl.BlockSpec(memory_space=pltpu.VMEM), pl.BlockSpec(memory_space=pl.ANY)
    slots = (4, 4, 4, CAP, WIDTH)
    sds = jax.ShapeDtypeStruct
    dma = pltpu.SemaphoreType.DMA
    results = pl.pallas_call(
        kernel,
        out_shape=(
            sds((ROWS, WIDTH), BF), sds((ROWS, WIDTH), BF),
            sds((QUARTER, FULL), BF), sds((HID, QUARTER), BF),
            sds((QUARTER, FULL), BF), sds((HID, QUARTER), BF),
            sds(slots, BF), sds(slots, BF), sds(slots, BF), sds(slots, BF),
        ),
        in_specs=[pl.BlockSpec(memory_space=pltpu.SMEM), anywhere, vmem, vmem] + [anywhere] * 3,
        out_specs=(anywhere,) * 10,
        scratch_shapes=[
            pltpu.VMEM((4, ROWS, WIDTH), BF), pltpu.VMEM((4, ROWS, WIDTH), BF),
            pltpu.VMEM(slots, BF), pltpu.VMEM(slots, BF),
            pltpu.VMEM(slots, BF), pltpu.VMEM(slots, BF),
            pltpu.VMEM((WIDTH, FULL), BF), pltpu.VMEM((HID, WIDTH), BF),
            pltpu.VMEM((1024, HID), BF), pltpu.VMEM((1024, FULL), BF),
            pltpu.VMEM(slots, BF), pltpu.VMEM(slots, BF),
            pltpu.VMEM((3, ROWS, WIDTH), BF), pltpu.VMEM((3, ROWS, WIDTH), BF),
            pltpu.VMEM((2, QUARTER, FULL), BF), pltpu.VMEM((2, HID, QUARTER), BF),
            pltpu.VMEM((QUARTER, FULL), BF), pltpu.VMEM((HID, QUARTER), BF),
            pltpu.VMEM((WIDTH, FULL), BF),
            pltpu.VMEM((3, 4, ROWS, 128), BF),
            pltpu.VMEM((MASKS, 4, ROWS, 256), BF),
            dma((12, 3)), dma((12, 3)), dma((3,)), dma((3,)), dma((2,)),
            dma((16,)), dma((16,)), dma((10,)),
        ],
        compiler_params=pltpu.CompilerParams(
            collective_id=0, has_side_effects=True, vmem_limit_bytes=64 * 2**20 - 2**16
        ),
        cost_estimate=pl.CostEstimate(flops=27 * 10**9, bytes_accessed=40 * 10**6, transcendentals=10**6),
    )(moving_slot, tokens, routes.T, gates.T, out_grad, expert_gate_up, expert_down)
    return pl.pallas_call(
        place,
        out_shape=(
            sds((ROWS, WIDTH), BF), sds((ROWS, WIDTH), BF),
            sds((2, QUARTER, FULL), BF), sds((2, HID, QUARTER), BF),
        ),
        in_specs=[pl.BlockSpec(memory_space=pltpu.SMEM)] + [anywhere] * 6,
        out_specs=(anywhere,) * 4,
        scratch_shapes=[
            pltpu.VMEM((2, ROWS, WIDTH), BF), pltpu.VMEM((2, QUARTER, FULL), BF),
            pltpu.VMEM((2, HID, QUARTER), BF), dma((8,)), dma((8,)),
        ],
    )(moving_slot, *results[:6])


def solution(mesh):
    rows, whole = P(("dp", "expert"), None), P("expert", None, None)
    return jax.shard_map(
        on_device,
        mesh=mesh,
        in_specs=(rows, rows, rows, rows, whole, whole, P()),
        out_specs=(rows, rows, P("expert", "dp", None), P("expert", None, "dp")),
        check_vma=False,
    )
```

```python
import jax
import jax.numpy as jnp
from jax import lax
from jax.experimental import pallas as pl
from jax.experimental.pallas import tpu as pltpu
from jax.sharding import PartitionSpec as P

MESH = pl.DeviceIdType.MESH
BF, F32 = jnp.bfloat16, jnp.float32

ROWS, WIDTH, HID, TOP, CAP = 128, 2048, 704, 6, 16
FULL = 2 * HID
QUARTER = WIDTH // 4

OUTBOUND = (
    ((0, 1, 2, 0, 640), (1, 2, 0, 640, 640), (2, 0, 1, 1280, 768)),
    ((0, 1, 2, 0, 768), (1, 2, 0, 768, 640), (2, 0, 1, 1408, 640)),
)
INBOUND = ((0, 1, 2, 0, 640), (1, 2, 0, 640, 896), (2, 0, 1, 1536, 512))

SCHEDULE = (
    "rows_home", "turn1", "to_core", "to_core", "kept0", "across", "across", "across", "kept1",
    "turn2", "finish1", "relocate", "across", "relocate", "across", "relocate", "across",
    "finish2", "relocate", "relocate", "relocate",
)
MASKS = len({chunk[:3] for chunk in OUTBOUND[0] + OUTBOUND[1] + INBOUND})


def device_at(x, y, z, core):
    return ((y // 2) * 2 + core, x * 8 + (y % 2) * 4 + z)


def dot(a, b, contract):
    return lax.dot_general(a, b, ((contract[:1], contract[1:]), ((), ())), preferred_element_type=F32)


def kernel(
    moving, tokens, routes, gates, out_grad, gate_up, down,
    mixed, token_grad, stay_gu, stay_dn, got_gu, got_dn, fwd1, fwd2, bck1, bck2,
    near1, near2, pick1, pick2, slot1, slot2, w_gu, w_dn, hid, pre_grad,
    back1, back2, part1, part2, core_gu, core_dn, lane_gu, lane_dn, g_gu, info, gated,
    sends, recvs, info_send, info_recv, w_sem, grad_send, grad_recv, out_sem,
):
    dp, ex = lax.axis_index("dp"), lax.axis_index("expert")
    y_hi, core = dp // 2, dp % 2
    me = (ex // 8, y_hi * 2 + (ex // 4) % 2, ex % 4)

    def along(axis, step):
        place = list(me)
        place[axis] = (place[axis] + step) % 4
        return device_at(*place, core)

    other_core = device_at(*me, 1 - core)

    barrier = pltpu.get_barrier_semaphore()
    for axis in range(3):
        for step in (1, 2, 3):
            pl.semaphore_signal(barrier, inc=1, device_id=along(axis, step), device_id_type=MESH)
    pl.semaphore_signal(barrier, inc=1, device_id=other_core, device_id_type=MESH)

    load_gu = pltpu.make_async_copy(gate_up.at[y_hi], w_gu, w_sem.at[0])
    load_dn = pltpu.make_async_copy(down.at[y_hi], w_dn, w_sem.at[1])
    load_gu.start()
    load_dn.start()

    def send(src, dst, send_sem, recv_sem, device):
        copy = pltpu.make_async_remote_copy(
            src_ref=src, dst_ref=dst, send_sem=send_sem, recv_sem=recv_sem,
            device_id=device, device_id_type=MESH,
        )
        copy.start()
        return copy

    def keep(src, dst, sem):
        copy = pltpu.make_async_copy(src, dst, sem)
        copy.start()
        return copy

    def wait_all(copies):
        for copy in copies:
            copy.wait()

    def group(sent, received, send_sem, recv_sem):
        return [
            pltpu.make_async_copy(received, received, recv_sem),
            pltpu.make_async_copy(sent, sent, send_sem),
        ]

    def fixed(axis, index, ref, columns):
        spot = [slice(None)] * 3
        spot[axis] = index
        return ref.at[(*spot, slice(None), columns)]

    def gather_axis(stage, source, near):
        started = []
        for q, (a, _, _, first, count) in enumerate(OUTBOUND[stage % 2]):
            columns = pl.ds(first, count)
            sems = sends.at[stage, q], recvs.at[stage, q]
            for step in (1, 3, 2):
                send(source.at[:, columns], near.at[step, :, columns], *sems, along(a, step))
            whole = near.at[pl.ds(1, 3), :, columns]
            started.append(group(whole, whole, *sems))
        return started

    own_rows = [keep(tokens, near1.at[0], out_sem.at[6]), keep(out_grad, near2.at[0], out_sem.at[7])]

    line = lax.broadcasted_iota(jnp.int32, (128, ROWS), 0)
    name = line % 64
    hits = jnp.zeros((128, ROWS), F32)
    weight = jnp.zeros((128, ROWS), F32)
    all_routes, all_gates = routes[...], gates[...].astype(F32)
    for k in range(TOP):
        same = all_routes[k : k + 1] == name
        hits = hits + jnp.where(same, 1.0, 0.0)
        weight = weight + jnp.where(same, all_gates[k : k + 1], 0.0)
    earlier = lax.broadcasted_iota(jnp.int32, (ROWS, ROWS), 0) < lax.broadcasted_iota(
        jnp.int32, (ROWS, ROWS), 1
    )
    rank = dot(hits.astype(BF), jnp.where(earlier, 1.0, 0.0).astype(BF), (1, 0))
    own_info = jnp.where(line < 64, jnp.where(hits > 0.5, rank, 99.0), weight).astype(BF)
    for axis in range(3):
        info[axis, 0] = own_info
    pl.semaphore_wait(barrier, 10)
    info_copies = []
    for axis in range(3):
        sems = info_send.at[axis], info_recv.at[axis]
        for step in (1, 3, 2):
            send(info.at[axis, 0], info.at[axis, step], *sems, along(axis, step))
        whole = info.at[axis, pl.ds(1, 3)]
        info_copies.append(group(whole, whole, *sems))
    gather1 = gather_axis(0, tokens, near1)
    wait_all(own_rows)

    def pick_masks(number_of, axis, b, c):
        row = lax.broadcasted_iota(jnp.int32, (128, 256), 0)
        column = lax.broadcasted_iota(jnp.int32, (128, 256), 1)
        place = [None, None, None]
        place[axis], place[b], place[c] = me[axis], column // 64, (column // 16) % 4
        expert = 2 * (place[0] * 8 + (place[1] % 2) * 4 + place[2]) + place[1] // 2
        choose_rank = jnp.where(row == expert, 1.0, 0.0).astype(BF)
        choose_gate = jnp.where(row == expert + 64, 1.0, 0.0).astype(BF)
        number = (lax.broadcasted_iota(jnp.int32, (ROWS, 256), 1) % 16).astype(F32)

        def one(step, _):
            ranks = dot(info[axis, step], choose_rank, (0, 0))
            scale = dot(info[axis, step], choose_gate, (0, 0))
            live = ranks == number
            gated[number_of, step] = jnp.where(live, scale, 0.0).astype(BF)
            return 0

        lax.fori_loop(0, 4, one, 0)

    def mask_of(which, step, with_gate):
        mask = gated[which, step]
        return mask if with_gate else jnp.where(mask.astype(F32) != 0.0, 1.0, 0.0).astype(BF)

    def pick(chunk, near, with_gate, picked):
        a, b, c, first, count = chunk
        which = masks[a, b, c]

        def one(step, _):
            rows = dot(mask_of(which, step, with_gate), near[step, :, first : first + count], (0, 0))
            source = (me[a] - step + 4) % 4
            picked[:, :, source, :, first : first + count] = rows.astype(BF).reshape(4, 4, 16, count)
            return 0

        lax.fori_loop(0, 4, one, 0)

    def quarters_of(buffer, columns, sems):
        return group(
            buffer.at[pl.ds(0, 3), :, :, :, columns], buffer.at[:, :, :, :, columns], *sems
        )

    def second_axis(stage, q, picked, onward):
        a, b, _, first, count = OUTBOUND[stage % 2][q]
        columns = pl.ds(first, count)
        landing = (
            onward.at[:, :, me[b], :, columns] if a < b else onward.at[:, me[b], :, :, columns]
        )
        sems = sends.at[stage, q], recvs.at[stage, q]
        for step in (1, 3, 2):
            send(picked.at[(me[b] + step) % 4, :, :, :, columns], landing, *sems, along(b, step))
        keep(picked.at[me[b], :, :, :, columns], landing, sems[1])
        return quarters_of(onward, columns, sems)

    def third_axis(stage, q, onward, slots):
        _, _, c, first, count = OUTBOUND[stage % 2][q]
        columns = pl.ds(first, count)
        landing = fixed(c, me[c], slots, columns)
        sems = sends.at[stage, q], recvs.at[stage, q]
        for step in (1, 3, 2):
            send(onward.at[(me[c] + step) % 4, :, :, :, columns], landing, *sems, along(c, step))
        keep(onward.at[me[c], :, :, :, columns], landing, sems[1])
        return quarters_of(slots, columns, sems)

    spread1, spread2, final1, final2 = [], [], [], []
    for copies in info_copies:
        wait_all(copies)
    masks = {}
    for axis, b, c in sorted({chunk[:3] for chunk in OUTBOUND[0] + OUTBOUND[1] + INBOUND}):
        masks[axis, b, c] = len(masks)
        pick_masks(masks[axis, b, c], axis, b, c)
    gather2 = gather_axis(1, out_grad, near2)
    for q, chunk in enumerate(OUTBOUND[0]):
        wait_all(gather1[q])
        pick(chunk, near1, False, pick1)
        spread1.append(second_axis(2, q, pick1, fwd1))
    for q, chunk in enumerate(OUTBOUND[1]):
        wait_all(gather2[q])
        pick(chunk, near2, True, pick2)
        spread2.append(second_axis(3, q, pick2, fwd2))
    for q in range(len(OUTBOUND[0])):
        wait_all(spread1[q])
        final1.append(third_axis(4, q, fwd1, slot1))
    for q in range(len(OUTBOUND[1])):
        wait_all(spread2[q])
        final2.append(third_axis(5, q, fwd2, slot2))

    load_gu.wait()
    load_dn.wait()
    for copies in final1:
        wait_all(copies)

    def forward(m, _):
        rows = slot1[m].reshape(256, WIDTH)
        projected = dot(rows, w_gu[...], (1, 0))
        here = pl.ds(pl.multiple_of(m * 256, 256), 256)
        pre_gate = projected[:, :HID]
        pre_up = projected[:, HID:]
        sigmoid_gate = jax.nn.sigmoid(pre_gate)
        activated = pre_gate * sigmoid_gate
        hidden = (activated * pre_up).astype(BF)
        hid[here] = hidden
        by_gate = pre_up * sigmoid_gate * (1.0 + pre_gate * (1.0 - sigmoid_gate))
        pre_grad[here] = jnp.concatenate([by_gate, activated], axis=1).astype(BF)
        pick1[m] = dot(hidden, w_dn[...], (1, 0)).astype(BF).reshape(4, 4, 16, WIDTH)
        return 0

    lax.fori_loop(0, 4, forward, 0)

    def first_back(stage, result, onward):
        started = []
        for q, (_, _, c, first, count) in enumerate(INBOUND):
            columns = pl.ds(first, count)
            landing = onward.at[me[c], :, :, :, columns]
            sems = sends.at[stage, q], recvs.at[stage, q]
            for step in (1, 3, 2):
                send(fixed(c, (me[c] + step) % 4, result, columns), landing, *sems, along(c, step))
            keep(fixed(c, me[c], result, columns), landing, sems[1])
            started.append(quarters_of(onward, columns, sems))
        return started

    def second_back(stage, q, onward, back):
        a, b, _, first, count = INBOUND[q]
        columns = pl.ds(first, count)

        def to(index):
            return onward.at[:, :, index, :, columns] if a < b else onward.at[:, index, :, :, columns]

        landing = back.at[me[b], :, :, :, columns]
        sems = sends.at[stage, q], recvs.at[stage, q]
        for step in (1, 3, 2):
            send(to((me[b] + step) % 4), landing, *sems, along(b, step))
        keep(to(me[b]), landing, sems[1])
        return quarters_of(back, columns, sems)

    def combine(stage, q, back, with_gate, near, part):
        a, b, c, first, count = INBOUND[q]
        which = masks[a, b, c]

        def one(step, _):
            target = (me[a] + step) % 4
            rows = back[:, :, target, :, first : first + count].reshape(256, count)
            near[step, :, first : first + count] = dot(
                mask_of(which, (4 - step) % 4, with_gate), rows, (1, 0)
            ).astype(BF)
            return 0

        lax.fori_loop(0, 4, one, 0)
        columns = pl.ds(first, count)
        sems = sends.at[stage, q], recvs.at[stage, q]
        for step in (1, 3, 2):
            send(near.at[step, :, columns], part.at[step - 1, :, columns], *sems, along(a, step))
        whole = part.at[:, :, columns]
        return group(whole, whole, *sems)

    home1 = first_back(6, pick1, bck1)

    for copies in final2:
        wait_all(copies)

    def backward(m, _):
        scaled = slot2[m].reshape(256, WIDTH)
        hidden_grad = dot(scaled, w_dn[...], (1, 1))
        here = pl.ds(pl.multiple_of(m * 256, 256), 256)
        twice = jnp.concatenate([hidden_grad, hidden_grad], axis=1)
        pre_grad[here] = (twice * pre_grad[here].astype(F32)).astype(BF)
        return 0

    def row_gradient(m, _):
        here = pl.ds(pl.multiple_of(m * 256, 256), 256)
        pick2[m] = dot(pre_grad[here], w_gu[...], (1, 1)).astype(BF).reshape(4, 4, 16, WIDTH)
        return 0

    lax.fori_loop(0, 4, backward, 0)

    quarters = [
        pl.multiple_of(QUARTER * (2 * hi + c), QUARTER)
        for c in (1 - core, core)
        for hi in (1 - y_hi, y_hi)
    ]

    def grad_gu(first, t, from_core, w_next):
        here = pl.ds(pl.multiple_of(first + t * 256, 256), 256)
        there = pl.ds(pl.multiple_of(t * 256, 256), 256)
        rows = slot1[:, :, :, :, here].reshape(1024, 256)
        result = dot(rows, pre_grad[...], (0, 0))
        if from_core is not None:
            result = result + core_gu[from_core, there].astype(F32)
        w_next[here] = result.astype(BF)

    def grad_dn(first, t, from_core, w_next):
        here = pl.ds(pl.multiple_of(first + t * 256, 256), 256)
        there = pl.ds(pl.multiple_of(t * 256, 256), 256)
        scaled = slot2[:, :, :, :, here].reshape(1024, 256)
        result = dot(hid[...], scaled, (0, 0))
        if from_core is not None:
            result = result + core_dn[from_core, :, there].astype(F32)
        w_next[:, here] = result.astype(BF)

    def gradients(first, from_core, w_gu_next, w_dn_next):
        def one(t, _):
            grad_gu(first, t, from_core, w_gu_next)
            grad_dn(first, t, from_core, w_dn_next)
            return 0

        lax.fori_loop(0, 2, one, 0)

    pieces = (("gu", 0, 128), ("gu", 128, 128), ("dn", 0, 256), ("gu", 256, 128), ("gu", 384, 128), ("dn", 256, 256))

    def piece_of(p, quarter, mine):
        kind, first, size = pieces[p]
        if kind == "gu":
            return (g_gu if mine else lane_gu), (pl.ds(pl.multiple_of(quarter + first, 64), size),)
        return (w_dn if mine else lane_dn), (slice(None), pl.ds(pl.multiple_of(quarter + first, 128), size))

    across, relocated, stayed = [], [], []

    def send_across(p):
        source, span = piece_of(p, quarters[2], True)
        target, there = piece_of(p, 0, False)
        across.append(send(
            source.at[span], target.at[there], grad_send.at[4 + p], grad_recv.at[4 + p], along(1, 2),
        ))

    moves_own = moving[ex] == y_hi

    def relocate(p):
        across[p].wait()
        held, span = piece_of(p, quarters[3], True)
        lane_held, there = piece_of(p, 0, False)
        mine, theirs = held[span], lane_held[there]
        out_span, stay_span = piece_of(p, quarters[0], True)[1], piece_of(p, quarters[1], True)[1]
        held[out_span] = jnp.where(moves_own, mine, theirs)
        held[stay_span] = jnp.where(moves_own, theirs, mine)
        got, stay = (got_gu, stay_gu) if pieces[p][0] == "gu" else (got_dn, stay_dn)
        relocated.append(send(
            held.at[out_span], got.at[there], grad_send.at[10 + p], grad_recv.at[10 + p], along(0, 2),
        ))
        stayed.append(keep(held.at[stay_span], stay.at[there], out_sem.at[p]))

    to_core, home2, turn1, turn2, last1, last2 = [], [], [], [], [], []

    def gradients_to_core():
        j = len(to_core)
        gradients(quarters[j], None, g_gu, w_dn)
        part_of = pl.ds(quarters[j], QUARTER)
        to_core.append([
            send(g_gu.at[part_of], core_gu.at[j], grad_send.at[2 * j], grad_recv.at[2 * j], other_core),
            send(w_dn.at[:, part_of], core_dn.at[j], grad_send.at[2 * j + 1],
                 grad_recv.at[2 * j + 1], other_core),
        ])

    def gradients_kept(j):
        wait_all(to_core[j])
        gradients(quarters[2 + j], j, g_gu, w_dn)

    def rows_home():
        lax.fori_loop(0, 4, row_gradient, 0)
        home2.extend(first_back(7, pick2, bck2))

    def turn(stage, home, onward, back, turned):
        for q in range(len(INBOUND)):
            wait_all(home[q])
            turned.append(second_back(stage, q, onward, back))

    def finish(stage, turned, back, with_gate, near, part, last):
        for q in range(len(INBOUND)):
            wait_all(turned[q])
            last.append(combine(stage, q, back, with_gate, near, part))

    steps = {
        "rows_home": rows_home,
        "turn1": lambda: turn(8, home1, bck1, back1, turn1),
        "turn2": lambda: turn(9, home2, bck2, back2, turn2),
        "finish1": lambda: finish(10, turn1, back1, True, near1, part1, last1),
        "finish2": lambda: finish(11, turn2, back2, False, near2, part2, last2),
        "to_core": gradients_to_core,
        "kept0": lambda: gradients_kept(0),
        "kept1": lambda: gradients_kept(1),
        "across": lambda: send_across(len(across)),
        "relocate": lambda: relocate(len(relocated)),
    }
    for step in SCHEDULE:
        steps[step]()

    def total(copies, near, part, result, sem):
        for q, (_, _, _, first, count) in enumerate(INBOUND):
            wait_all(copies[q])
            span = slice(first, first + count)
            summed = near[0, :, span].astype(F32)
            for step in range(3):
                summed = summed + part[step, :, span].astype(F32)
            near[0, :, span] = summed.astype(BF)
        return keep(near.at[0], result, out_sem.at[sem])

    stayed.append(total(last1, near1, part1, mixed, 8))
    stayed.append(total(last2, near2, part2, token_grad, 9))
    wait_all(stayed)
    wait_all(relocated)


def place(moving, mixed, token_grad, stay_gu, stay_dn, got_gu, got_dn,
          mixed_out, token_grad_out, gu_out, dn_out, rows_held, gu_held, dn_held, sem_in, sem_out):
    moved = moving[lax.axis_index("expert")]
    moves = [
        (mixed, rows_held.at[0], mixed_out), (token_grad, rows_held.at[1], token_grad_out),
    ]
    for i, (slot, gu, dn) in enumerate(((moved, got_gu, got_dn), (1 - moved, stay_gu, stay_dn))):
        for p in range(2):
            rows = pl.ds(p * 256, 256)
            moves.append((gu.at[rows], gu_held.at[i, rows], gu_out.at[slot, rows]))
        moves.append((dn, dn_held.at[i], dn_out.at[slot]))
    loads = [pltpu.make_async_copy(src, held, sem_in.at[i]) for i, (src, held, _) in enumerate(moves)]
    stores = [pltpu.make_async_copy(held, dst, sem_out.at[i]) for i, (_, held, dst) in enumerate(moves)]
    for copy in loads:
        copy.start()
    for load, store in zip(loads, stores):
        load.wait()
        store.start()
    for copy in stores:
        copy.wait()


def on_device(tokens, routes, gates, out_grad, expert_gate_up, expert_down, moving_slot):
    vmem, anywhere = pl.BlockSpec(memory_space=pltpu.VMEM), pl.BlockSpec(memory_space=pl.ANY)
    slots = (4, 4, 4, CAP, WIDTH)
    sds = jax.ShapeDtypeStruct
    dma = pltpu.SemaphoreType.DMA
    results = pl.pallas_call(
        kernel,
        out_shape=(
            sds((ROWS, WIDTH), BF), sds((ROWS, WIDTH), BF),
            sds((QUARTER, FULL), BF), sds((HID, QUARTER), BF),
            sds((QUARTER, FULL), BF), sds((HID, QUARTER), BF),
            sds(slots, BF), sds(slots, BF), sds(slots, BF), sds(slots, BF),
        ),
        in_specs=[pl.BlockSpec(memory_space=pltpu.SMEM), anywhere, vmem, vmem] + [anywhere] * 3,
        out_specs=(anywhere,) * 10,
        scratch_shapes=[
            pltpu.VMEM((4, ROWS, WIDTH), BF), pltpu.VMEM((4, ROWS, WIDTH), BF),
            pltpu.VMEM(slots, BF), pltpu.VMEM(slots, BF),
            pltpu.VMEM(slots, BF), pltpu.VMEM(slots, BF),
            pltpu.VMEM((WIDTH, FULL), BF), pltpu.VMEM((HID, WIDTH), BF),
            pltpu.VMEM((1024, HID), BF), pltpu.VMEM((1024, FULL), BF),
            pltpu.VMEM(slots, BF), pltpu.VMEM(slots, BF),
            pltpu.VMEM((3, ROWS, WIDTH), BF), pltpu.VMEM((3, ROWS, WIDTH), BF),
            pltpu.VMEM((2, QUARTER, FULL), BF), pltpu.VMEM((2, HID, QUARTER), BF),
            pltpu.VMEM((QUARTER, FULL), BF), pltpu.VMEM((HID, QUARTER), BF),
            pltpu.VMEM((WIDTH, FULL), BF),
            pltpu.VMEM((3, 4, ROWS, 128), BF),
            pltpu.VMEM((MASKS, 4, ROWS, 256), BF),
            dma((12, 3)), dma((12, 3)), dma((3,)), dma((3,)), dma((2,)),
            dma((16,)), dma((16,)), dma((10,)),
        ],
        compiler_params=pltpu.CompilerParams(
            collective_id=0, has_side_effects=True, vmem_limit_bytes=64 * 2**20 - 2**16
        ),
        cost_estimate=pl.CostEstimate(flops=27 * 10**9, bytes_accessed=40 * 10**6, transcendentals=10**6),
    )(moving_slot, tokens, routes.T, gates.T, out_grad, expert_gate_up, expert_down)
    return pl.pallas_call(
        place,
        out_shape=(
            sds((ROWS, WIDTH), BF), sds((ROWS, WIDTH), BF),
            sds((2, QUARTER, FULL), BF), sds((2, HID, QUARTER), BF),
        ),
        in_specs=[pl.BlockSpec(memory_space=pltpu.SMEM)] + [anywhere] * 6,
        out_specs=(anywhere,) * 4,
        scratch_shapes=[
            pltpu.VMEM((2, ROWS, WIDTH), BF), pltpu.VMEM((2, QUARTER, FULL), BF),
            pltpu.VMEM((2, HID, QUARTER), BF), dma((8,)), dma((8,)),
        ],
    )(moving_slot, *results[:6])


def solution(mesh):
    rows, whole = P(("dp", "expert"), None), P("expert", None, None)
    return jax.shard_map(
        on_device,
        mesh=mesh,
        in_specs=(rows, rows, rows, rows, whole, whole, P()),
        out_specs=(rows, rows, P("expert", "dp", None), P("expert", None, "dp")),
        check_vma=False,
    )
```
